32 devices in a mesh: gx: 4 (over z), gy: 2 (over x), gz: 4 (over y, core).
Axes of the slice: x: 2, y: 2, z: 4, core: 2. Of those that a mesh axis runs over, the one named last changes fastest.
Arguments:
- velocity: float32 [3, 64, 64, 256], P(None, 'gz', 'gx', 'gy'), may hold values from -20 to 20
- owner: int32 [32768, 1], P(('gx', 'gy', 'gz')), may hold values from 0 to 7; in each aligned block of 1024 rows (0 to 1023, 1024 to 2047, ...) at most 512 rows name the same one
- cell_x: int32 [32768], P(('gx', 'gy', 'gz')), may hold values from 0 to 14
- cell_y: int32 [32768], P(('gx', 'gy', 'gz')), may hold values from 0 to 126
- cell_z: int32 [32768], P(('gx', 'gy', 'gz')), may hold values from 0 to 14
- query_weights: float32 [3, 32768], P(None, ('gx', 'gy', 'gz')), may hold values from 0 to 1
Outputs:
- query_stress: float32 [6, 32768], P(None, ('gx', 'gy', 'gz'))
The draws below stay inside these ranges and needn't reach their ends.
Inputs may be any that keep to these rules, and one draw needn't show every extreme that they name: Among the queries held by one device, at most 512 name the same owner, and in every draw some owner is named by exactly 512 of them. `cell_x`: the corner cell plus one stays in the same brick.
All inputs are finite; a program needn't handle non-finite values.
Results may differ from the reference program's by a relative error of at most 0.0003.
Values sent between devices are 32-bit elements; how exact they have to be, the bound alone decides.
No kernel may reach another device: no remote copies, remote signals or barrier semaphores. Data moves between devices by JAX's collectives and lax.ppermute only.
A program may use at most 64 MiB of HBM per device.

```python
import math
import jax
import jax.numpy as jnp
import numpy as np
from jax import lax

CX = 16
CY = 128
CZ = 16
Q = 1024
FW = 32
NX = 64
NY = 256
NZ = 64
NQ = 32768
CAP = 512
N_GX = 4
N_GY = 2
N_GZ = 4


def draw_velocity(key, part):
    keys = jax.random.split(jax.random.fold_in(key, 17), 8)
    two_pi = 2.0 * math.pi
    zc = jnp.arange(NZ).astype(jnp.float32) * (two_pi / NZ)
    xc = jnp.arange(NX).astype(jnp.float32) * (two_pi / NX)
    yc = jnp.arange(NY).astype(jnp.float32) * (two_pi / NY)
    wave_z = jax.random.randint(keys[0], (3, 4), 0, 2).astype(jnp.float32)
    wave_x = jax.random.randint(keys[1], (3, 4), 1, 4).astype(jnp.float32)
    wave_y = jax.random.randint(keys[2], (3, 4), 1, 4).astype(jnp.float32)
    phases = jax.random.uniform(keys[3], (3, 4, 3), jnp.float32, 0.0, two_pi)
    amplitude = jax.random.uniform(keys[4], (3, 4), jnp.float32, -1.5, 1.5)
    large = jnp.zeros((3, NZ, NX, NY), jnp.float32)
    for mode in range(4):
        along_z = jnp.cos(wave_z[:, mode][:, None] * zc[None, :] + phases[:, mode, 0][:, None])
        along_x = jnp.cos(wave_x[:, mode][:, None] * xc[None, :] + phases[:, mode, 1][:, None])
        along_y = jnp.cos(wave_y[:, mode][:, None] * yc[None, :] + phases[:, mode, 2][:, None])
        large = large + amplitude[:, mode][:, None, None, None] * along_z[:, :, None, None] * along_x[:, None, :, None] * along_y[:, None, None, :]
    shift = jax.random.uniform(keys[5], (2,), jnp.float32, 0.0, two_pi)
    envelope = jnp.exp(0.5 * jnp.cos(xc + shift[0])[:, None] * jnp.cos(yc + shift[1])[None, :])
    noise = jnp.clip(jax.random.normal(keys[6], (3, NZ, NX, NY), jnp.float32), -4.0, 4.0)
    shared = jnp.clip(jax.random.normal(keys[7], (NZ, NX, NY), jnp.float32), -4.0, 4.0)
    return large + envelope[None, None] * (noise + 0.7 * shared[None])


def set_ends(array, own_key, least, high):
    place = [jax.random.randint(jax.random.fold_in(own_key, axis), (), 0, length) for axis, length in enumerate(array.shape)]
    widest = array.shape.index(max(array.shape))
    beside = place[:widest] + [(place[widest] + 1) % array.shape[widest]] + place[widest + 1:]
    return array.at[tuple(place)].set(least).at[tuple(beside)].set(high)


def steps_of(stream_key, dims, cuts, smallest, high):
    level, own = 1.0, jax.random.fold_in(stream_key, 6)
    for position, shards_of in cuts:
        draws = jnp.exp(jax.random.uniform(jax.random.fold_in(own, position), (shards_of,), jnp.float32, smallest / len(cuts), high / len(cuts)))
        level = level * jnp.repeat(draws, dims[position] // shards_of).reshape([-1 if axis == position else 1 for axis in range(len(dims))])
    return level


def routed_block(own_key, own, number, rows, number_of, top, bound, skew):
    order = jax.random.permutation(own_key, number_of)
    packed, usual = shares(number_of, rows * top, bound, skew, True), shares(number_of, rows * top, bound, skew, False)
    places = jnp.arange(number_of)

    def named(tallies, offset_by):
        used = int((tallies > 0).sum())
        fixed = max(1, used // 4)
        moved = fixed + (places - fixed + offset_by * (used - fixed)) % max(1, number_of - fixed)
        return jnp.zeros((number_of,), jnp.int32).at[order[jnp.where(places < fixed, places, moved)]].set(jnp.asarray(tallies, jnp.int32))

    tallies = jnp.where(number % 4 == 0, named(packed, number // 4), named(usual, number - number // 4 - 1))
    mixed = jax.random.permutation(jax.random.fold_in(own, 3), number_of)
    source_of, taker = mixed[0:number_of // 2 * 2:2], mixed[1:number_of // 2 * 2:2]
    slack = jnp.minimum(tallies[source_of] - 1, bound - tallies[taker]) // 2
    slack = jnp.where((source_of == order[0]) | (taker == order[0]) | (tallies[taker] == 0), 0, jnp.maximum(slack, 0))
    moved = jax.random.randint(jax.random.fold_in(own, 4), (number_of // 2,), 0, 1 << 20) % (slack + 1)
    tallies = tallies.at[source_of].add(-moved).at[taker].add(moved)
    members = jnp.searchsorted(jnp.cumsum(tallies), jnp.arange(rows * top), side="right").astype(jnp.int32)
    grid = members.reshape(top, rows).T
    grid = grid[jax.random.permutation(jax.random.fold_in(own, 1), rows)]
    offset_by = jax.random.randint(jax.random.fold_in(own, 2), (rows, 1), 0, top)
    return jnp.take_along_axis(grid, (jnp.arange(top)[None, :] + offset_by) % top, axis=1)


def shares(count, total, most, lean, full):
    loads = [(1 << 20) // math.isqrt(standing ** lean) + 1 for standing in range(1, count + 1)]
    largest = most if full else min(most, max(-(-total // count), total * loads[0] // sum(loads)))
    least = 1 if total - largest >= count - 1 else 0
    holding, surplus = [largest] + [least] * (count - 1), total - largest - least * (count - 1)
    while surplus > 0:
        candidates = [i for i in range(1, count) if holding[i] < largest] or [i for i in range(1, count) if holding[i] < most]
        mass, budget = sum([loads[i] for i in candidates]), surplus
        for i in candidates:
            extra = min(most - holding[i], max(1, budget * loads[i] // mass), surplus)
            holding[i] = holding[i] + extra
            surplus = surplus - extra
    return np.array(holding)


def setup_inputs(seed: int = 0) -> dict:
    key_of = jax.random.split(jax.random.key(seed), 7)
    velocity = draw_velocity(jax.random.fold_in(key_of[6], 71), 0)
    owner_keys = jax.random.split(jax.random.fold_in(key_of[1], 1), NQ // Q)
    owner_turns = jax.random.permutation(jax.random.fold_in(key_of[1], 3), NQ // Q)
    owner = jax.vmap(lambda own, number: routed_block(jax.random.fold_in(key_of[1], 2), own, number, Q, N_GX * N_GY, 1, CAP, 2))(owner_keys, owner_turns).reshape((NQ, 1))
    cell_x = set_ends(jax.random.randint(key_of[2], (NQ,), 0, CX - 1), jax.random.fold_in(key_of[2], 1), 0, (CX - 1) - 1).astype(jnp.int32)
    cell_y = set_ends(jax.random.randint(key_of[3], (NQ,), 0, CY - 1), jax.random.fold_in(key_of[3], 1), 0, (CY - 1) - 1).astype(jnp.int32)
    cell_z = set_ends(jax.random.randint(key_of[4], (NQ,), 0, CZ - 1), jax.random.fold_in(key_of[4], 1), 0, (CZ - 1) - 1).astype(jnp.int32)
    query_weights = jnp.clip(1.0 * jax.random.uniform(key_of[5], (3, NQ), jnp.float32) ** steps_of(key_of[5], (3, NQ), ((1, 32),), -0.2, 0.2), 0.0, 1.0)
    return {"velocity": velocity, "owner": owner, "cell_x": cell_x, "cell_y": cell_y, "cell_z": cell_z, "query_weights": query_weights}


PAIRS = ((0, 0), (0, 1), (0, 2), (1, 1), (1, 2), (2, 2))


def taps(radius, width):
    offsets = jnp.arange(2 * radius + 1).astype(jnp.float32) - radius
    values = jnp.exp(-6.0 * offsets * offsets / (width * width))
    return values / jnp.sum(values)


def band(length, radius, width):
    weights = taps(radius, width)
    rows = jnp.arange(length + 2 * radius)[:, None]
    cols = jnp.arange(length)[None, :]
    offset = rows - cols
    inside = (offset >= 0) & (offset <= 2 * radius)
    picked = weights[jnp.clip(offset, 0, 2 * radius)]
    return jnp.where(inside, picked, jnp.zeros_like(picked))


def filter_axis(field, axis, block, radius):
    length = field.shape[axis]
    upper = lax.slice_in_dim(field, length - radius, length, axis=axis)
    lower = lax.slice_in_dim(field, 0, radius, axis=axis)
    wide = jnp.concatenate([upper, field, lower], axis=axis)
    matrix = band(block, radius, FW).astype(field.dtype)
    pieces = []
    for number in range(length // block):
        window = lax.slice_in_dim(wide, number * block, number * block + block + 2 * radius, axis=axis)
        result = jnp.tensordot(window, matrix, axes=([axis], [0]), precision=lax.Precision.HIGHEST)
        pieces.append(jnp.moveaxis(result, -1, axis))
    return jnp.concatenate(pieces, axis=axis)


def smooth(field, radius):
    field = filter_axis(field, 0, CZ, radius)
    field = filter_axis(field, 1, CX, radius)
    return filter_axis(field, 2, CY, radius)


def reference(velocity, owner, cell_x, cell_y, cell_z, query_weights):
    radius = FW // 2
    means = [smooth(velocity[k], radius) for k in range(3)]
    holder = jnp.arange(NQ).astype(jnp.int32) // Q
    brick_z = holder % N_GZ
    brick = owner[:, 0]
    glob_x = (brick // N_GY) * CX + cell_x
    glob_y = (brick % N_GY) * CY + cell_y
    glob_z = brick_z * CZ + cell_z
    base = (glob_z * NX + glob_x) * NY + glob_y
    wx = query_weights[0]
    wy = query_weights[1]
    wz = query_weights[2]
    rows = []
    for first, second in PAIRS:
        stress = smooth(velocity[first] * velocity[second], radius) - means[first] * means[second]
        flat = stress.reshape(-1)
        total = jnp.zeros((NQ,), stress.dtype)
        for dz in (0, 1):
            for dx in (0, 1):
                for dy in (0, 1):
                    index = base + dz * NX * NY + dx * NY + dy
                    term = (wz if dz else 1.0 - wz) * (wx if dx else 1.0 - wx) * (wy if dy else 1.0 - wy)
                    total = total + term * flat[index]
        rows.append(total)
    return jnp.stack(rows)
```

```python
import jax
import jax.numpy as jnp
from jax import lax
from jax.sharding import PartitionSpec as P

FW = 32


PAIRS = ((0, 0), (0, 1), (0, 2), (1, 1), (1, 2), (2, 2))


def padded(x, sides, width):
    for axis, dim in sides:
        devices, length = (lax.axis_size(axis), x.shape[dim])
        up = [(i, (i + 1) % devices) for i in range(devices)]
        down = [(j, i) for i, j in up]
        last = lax.slice_in_dim(x, length - width, length, axis=dim)
        initial = lax.slice_in_dim(x, 0, width, axis=dim)
        before = lax.ppermute(last, axis, up)
        after = lax.ppermute(initial, axis, down)
        x = jnp.concatenate([before, x, after], axis=dim)
    return x


def taps(radius, width):
    offsets = jnp.arange(2 * radius + 1).astype(jnp.float32) - radius
    values = jnp.exp(-6.0 * offsets * offsets / (width * width))
    return values / jnp.sum(values)


def band(length, radius, width):
    weights = taps(radius, width)
    rows = jnp.arange(length + 2 * radius)[:, None]
    cols = jnp.arange(length)[None, :]
    offset = rows - cols
    inside = (offset >= 0) & (offset <= 2 * radius)
    picked = weights[jnp.clip(offset, 0, 2 * radius)]
    return jnp.where(inside, picked, jnp.zeros_like(picked))


def filter_x(fields, matrix):
    return jnp.einsum("czpy,pq->czqy", fields, matrix, precision=lax.Precision.HIGHEST)


def filter_y(fields, matrix):
    return jnp.einsum("czxp,pq->czxq", fields, matrix, precision=lax.Precision.HIGHEST)


def interpolate(flat_stress, index, weight, size_x, size_y):
    shape = index.shape[1:]
    base = index[0].reshape(-1)
    offsets = weight.reshape(3, -1)
    wx = offsets[0]
    wy = offsets[1]
    wz = offsets[2]
    total = jnp.zeros((6, base.shape[0]), jnp.float32)
    for dz in (0, 1):
        for dx in (0, 1):
            for dy in (0, 1):
                corner = base + dz * size_x * size_y + dx * size_y + dy
                values = jnp.take(flat_stress, corner, axis=1)
                term = (
                    (wz if dz else 1.0 - wz) * (wx if dx else 1.0 - wx) * (wy if dy else 1.0 - wy)
                )
                total = total + term[None, :] * values
    return total.reshape((6,) + shape)


def on_device(velocity, owner, cell_x, cell_y, cell_z, query_weights):
    radius = FW // 2
    size_z = velocity.shape[1]
    size_x = velocity.shape[2]
    size_y = velocity.shape[3]
    layered = padded(velocity, (("gz", 1),), radius)
    band_z = band(size_z, radius, FW)
    band_x = band(size_x, radius, FW)
    band_y = band(size_y, radius, FW)
    fields = []
    for comp in range(3):
        fields.append(
            jnp.einsum("pxy,pz->zxy", layered[comp], band_z, precision=lax.Precision.HIGHEST)
        )
    for first, second in PAIRS:
        product = layered[first] * layered[second]
        fields.append(jnp.einsum("pxy,pz->zxy", product, band_z, precision=lax.Precision.HIGHEST))
    stacked = jnp.stack(fields)
    margin_x = padded(stacked, (("gx", 2),), radius)
    along_x = filter_x(margin_x, band_x)
    margin_y = padded(along_x, (("gy", 3),), radius)
    filtered = filter_y(margin_y, band_y)
    stress = jnp.stack(
        [
            filtered[3 + k] - filtered[first] * filtered[second]
            for k, (first, second) in enumerate(PAIRS)
        ]
    )
    flat_stress = stress.reshape(6, -1)
    bricks_x = lax.axis_size("gx")
    bricks_y = lax.axis_size("gy")
    owners = bricks_x * bricks_y
    count = owner.shape[0]
    capacity = 4 * count // owners
    target = owner[:, 0]
    order = jnp.argsort(target, stable=True)
    sorted_target = target[order]
    tally = jnp.sum(
        (target[:, None] == jnp.arange(owners, dtype=jnp.int32)[None, :]).astype(jnp.int32), axis=0
    )
    earlier = jnp.arange(owners)[None, :] < jnp.arange(owners)[:, None]
    starts = jnp.sum(jnp.where(earlier, tally[None, :], 0), axis=1)
    sorted_rank = jnp.arange(count, dtype=jnp.int32) - starts[sorted_target]
    rank = jnp.zeros((count,), jnp.int32).at[order].set(sorted_rank)
    slot = target * capacity + rank
    local_cell = (cell_z * size_x + cell_x) * size_y + cell_y
    send_index = jnp.zeros((owners * capacity,), jnp.int32).at[slot].set(local_cell)
    send_weight = jnp.zeros((3, owners * capacity), jnp.float32).at[:, slot].set(query_weights)
    values = interpolate(
        flat_stress,
        lax.all_to_all(
            send_index.reshape(1, owners, capacity),
            ("gx", "gy"),
            split_axis=1,
            concat_axis=1,
            tiled=True,
        ),
        lax.all_to_all(
            send_weight.reshape(3, owners, capacity),
            ("gx", "gy"),
            split_axis=1,
            concat_axis=1,
            tiled=True,
        ),
        size_x,
        size_y,
    )
    returned = lax.all_to_all(values, ("gx", "gy"), split_axis=1, concat_axis=1, tiled=True)
    flat_back = returned.reshape(6, owners * capacity)
    return jnp.take(flat_back, slot, axis=1)


def solution(mesh):
    placed = (
        P(None, "gz", "gx", "gy"),
        P(("gx", "gy", "gz"), None),
        P(("gx", "gy", "gz")),
        P(("gx", "gy", "gz")),
        P(("gx", "gy", "gz")),
        P(None, ("gx", "gy", "gz")),
    )
    return jax.shard_map(
        on_device,
        mesh=mesh,
        in_specs=placed,
        out_specs=P(None, ("gx", "gy", "gz")),
        check_vma=False,
    )
```

```python
import math

import jax
import jax.numpy as jnp
import numpy as np
from jax import lax
from jax.experimental import pallas as pl
from jax.experimental.pallas import tpu as pltpu
from jax.sharding import PartitionSpec as P

FW = 32
PAIRS = ((0, 0), (0, 1), (0, 2), (1, 1), (1, 2), (2, 2))
ROWS = 8
F32 = jnp.float32
BF16 = jnp.bfloat16
WHOLE = pl.BlockSpec(memory_space=pltpu.VMEM)
PARAMS = pltpu.CompilerParams(vmem_limit_bytes=48 * 1024 * 1024)


def taps():
    radius = FW // 2
    values = [math.exp(-6.0 * (m - radius) ** 2 / FW**2) for m in range(2 * radius + 1)]
    return [v / sum(values) for v in values]


def neighbours(x, axis):
    devices = lax.axis_size(axis)
    up = [(i, (i + 1) % devices) for i in range(devices)]
    down = [(j, i) for i, j in up]
    return lax.ppermute(x, axis, up), lax.ppermute(x, axis, down)


def symmetric(values, centre):
    radius = FW // 2
    g = taps()
    total = g[radius] * values[centre]
    for m in range(1, radius + 1):
        total = total + g[radius + m] * (values[centre - m] + values[centre + m])
    return total


def split2(x):
    high = x.astype(BF16)
    return high, (x - high.astype(F32)).astype(BF16)


def split3(x):
    high, rest = x.astype(BF16), None
    rest = x - high.astype(F32)
    middle = rest.astype(BF16)
    return high, middle, (rest - middle.astype(F32)).astype(BF16)


def z_kernel(before, own, after, out, wide):
    layers, size_x = own.shape[1], own.shape[2]
    radius = FW // 2

    for part, (ref, skip) in enumerate(((before, layers - radius), (own, 0), (after, 0))):
        place = (0, radius, radius + layers)[part]

        def products(z, carry, ref=ref, skip=skip, place=place):
            u = [ref[k, z + skip] for k in range(3)]
            for k in range(3):
                wide[k, z + place] = u[k]
            for k, (a, b) in enumerate(PAIRS):
                wide[3 + k, z + place] = u[a] * u[b]
            return carry

        lax.fori_loop(0, layers if part == 1 else radius, products, 0)

    def filtered(f, carry):
        for x in range(0, size_x, 8):
            values = [wide[f, z, x : x + 8] for z in range(layers + 2 * radius)]
            for z in range(layers):
                out[f, z, x : x + 8] = symmetric(values, z + radius)
        return carry

    lax.fori_loop(0, 9, filtered, 0)


def along_z(before, own, after):
    _, z, x, y = own.shape
    return pl.pallas_call(
        z_kernel,
        out_shape=jax.ShapeDtypeStruct((9, z, x, y), F32),
        in_specs=[WHOLE] * 3,
        out_specs=WHOLE,
        scratch_shapes=[pltpu.VMEM((9, z + FW, x, y), F32)],
        compiler_params=PARAMS,
        cost_estimate=pl.CostEstimate(flops=9 * z * x * y * 66, bytes_accessed=21 * z * x * y * 4, transcendentals=0),
    )(before, own, after)


def x_kernel(before, own, after, out, strips, wide):
    layers, size_x, size_y = own.shape[1:]
    radius = FW // 2

    def filtered(n, carry):
        f, z = n // layers, n % layers
        wide[0:radius] = before[f, z, size_x - radius :]
        wide[radius : radius + size_x] = own[f, z]
        wide[radius + size_x :] = after[f, z, :radius]
        values = [wide[i : i + 8] for i in range(size_x + FW - 7)]
        for x in range(0, size_x, 8):
            total = symmetric(values, x + radius)
            row = pl.ds(pl.multiple_of(z * size_x, 8) + x, 8)
            out[f, row] = total
            strips[f, row, :radius] = total[:, :radius]
            strips[f, row, radius:] = total[:, size_y - radius :]
        return carry

    lax.fori_loop(0, 9 * layers, filtered, 0)


def along_x(before, own, after):
    _, z, x, y = own.shape
    return pl.pallas_call(
        x_kernel,
        out_shape=(
            jax.ShapeDtypeStruct((9, z * x, y), F32),
            jax.ShapeDtypeStruct((9, z * x, FW), F32),
        ),
        in_specs=[WHOLE] * 3,
        out_specs=(WHOLE, WHOLE),
        scratch_shapes=[pltpu.VMEM((x + FW, y), F32)],
        compiler_params=PARAMS,
        cost_estimate=pl.CostEstimate(flops=9 * z * x * y * 66, bytes_accessed=40 * z * x * y * 4, transcendentals=0),
    )(before, own, after)


def sample_kernel(own, strips, band, w_high, w_low, w_y, out, field_high, field_low):
    cells, size_y = own.shape[1:]

    def smooth(f):
        a = lax.dot_general(
            band[:, :size_y], own[f], (((1,), (1,)), ((), ())),
            precision=lax.Precision.HIGHEST, preferred_element_type=F32,
        )
        b = lax.dot_general(
            band[:, size_y:], strips[f], (((1,), (1,)), ((), ())),
            precision=lax.Precision.HIGHEST, preferred_element_type=F32,
        )
        return a + b

    mean = [smooth(k) for k in range(3)]
    for k, (a, b) in enumerate(PAIRS):
        high, low = split2(smooth(3 + k) - mean[a] * mean[b])
        field_high[k * size_y : (k + 1) * size_y] = high
        field_low[k * size_y : (k + 1) * size_y] = low

    count = w_y.shape[1]
    block = min(count, 256)

    def sample(n, carry):
        here = pl.ds(pl.multiple_of(n * block, block), block)
        wide = jnp.dot(field_high[...], w_high[:, here], preferred_element_type=F32)
        wide = wide + jnp.dot(field_low[...], w_high[:, here], preferred_element_type=F32)
        wide = wide + jnp.dot(field_high[...], w_low[:, here], preferred_element_type=F32)
        weight = w_y[:, here]
        for k in range(6):
            out[k : k + 1, here] = jnp.sum(wide[k * size_y : (k + 1) * size_y] * weight, axis=0, keepdims=True)
        out[6:8, here] = jnp.zeros((2, block), F32)
        return carry

    lax.fori_loop(0, count // block, sample, 0)


def samples(own, strips, band, w_high, w_low, w_y):
    cells, size_y = own.shape[1:]
    count = w_y.shape[1]
    return pl.pallas_call(
        sample_kernel,
        out_shape=jax.ShapeDtypeStruct((ROWS, count), F32),
        in_specs=[WHOLE] * 6,
        out_specs=WHOLE,
        scratch_shapes=[pltpu.VMEM((6 * size_y, cells), BF16), pltpu.VMEM((6 * size_y, cells), BF16)],
        compiler_params=PARAMS,
        cost_estimate=pl.CostEstimate(flops=6 * size_y * cells * count * 6, bytes_accessed=8 * 1024 * 1024, transcendentals=0),
    )(own, strips, band, w_high, w_low, w_y)


def route_kernel(owners, capacity, owner, cells, weights, out, rank_out):
    count = owner.shape[1]
    target = owner[...]
    named = lax.broadcasted_iota(jnp.int32, (owners, count), 0) == target
    earlier = lax.broadcasted_iota(jnp.int32, (count, count), 0) < lax.broadcasted_iota(jnp.int32, (count, count), 1)
    before = jnp.dot(
        jnp.where(named, 1.0, 0.0).astype(BF16), jnp.where(earlier, 1.0, 0.0).astype(BF16),
        preferred_element_type=F32,
    )
    rank = jnp.sum(jnp.where(named, before, 0.0), axis=0, keepdims=True).astype(jnp.int32)
    rank_out[...] = rank
    slot = lax.broadcasted_iota(jnp.int32, (capacity, count), 0) == rank
    slot = jnp.where(slot, 1.0, 0.0).astype(BF16)
    record = jnp.concatenate(
        [cells[...].astype(F32), weights[...], jnp.zeros((ROWS - 6, count), F32)], axis=0
    )
    total = jnp.zeros((owners * ROWS, capacity), F32)
    for part in split3(record):
        part = part.astype(F32)
        spread = jnp.concatenate(
            [jnp.where(target == o, part, 0.0) for o in range(owners)], axis=0
        ).astype(BF16)
        total = total + lax.dot_general(spread, slot, (((1,), (1,)), ((), ())), preferred_element_type=F32)
    out[...] = total


def route(owner, cells, weights, owners, capacity):
    count = owner.shape[1]

    def kernel(*refs):
        route_kernel(owners, capacity, *refs)

    return pl.pallas_call(
        kernel,
        out_shape=(
            jax.ShapeDtypeStruct((owners * ROWS, capacity), F32),
            jax.ShapeDtypeStruct((1, count), jnp.int32),
        ),
        in_specs=[WHOLE] * 3,
        out_specs=(WHOLE, WHOLE),
        compiler_params=PARAMS,
        cost_estimate=pl.CostEstimate(flops=10 * count * count * owners, bytes_accessed=count * 4 * 40, transcendentals=0),
    )(owner, cells, weights)


def hat_kernel(size_x, size_z, size_y, asked, w_high, w_low, w_y):
    def hat(size, row, offset):
        distance = lax.broadcasted_iota(jnp.int32, (size, asked.shape[1]), 0) - row.astype(jnp.int32)
        return jnp.where(distance == 0, 1.0 - offset, jnp.where(distance == 1, offset, 0.0))

    in_z = hat(size_z, asked[0:1], asked[5:6])
    in_x = hat(size_x, asked[1:2], asked[3:4])
    w_y[...] = hat(size_y, asked[2:3], asked[4:5])
    for z in range(size_z):
        high, low = split2(in_z[z : z + 1] * in_x)
        w_high[z * size_x : (z + 1) * size_x] = high
        w_low[z * size_x : (z + 1) * size_x] = low


def hats(asked, size_z, size_x, size_y):
    count = asked.shape[1]
    block = 512

    def kernel(*refs):
        hat_kernel(size_x, size_z, size_y, *refs)

    def columns(rows):
        return pl.BlockSpec((rows, block), lambda n: (0, n))

    return pl.pallas_call(
        kernel,
        grid=(count // block,),
        out_shape=(
            jax.ShapeDtypeStruct((size_z * size_x, count), BF16),
            jax.ShapeDtypeStruct((size_z * size_x, count), BF16),
            jax.ShapeDtypeStruct((size_y, count), F32),
        ),
        in_specs=[columns(ROWS)],
        out_specs=(columns(size_z * size_x), columns(size_z * size_x), columns(size_y)),
        compiler_params=PARAMS,
        cost_estimate=pl.CostEstimate(flops=count * 2000, bytes_accessed=count * 1600, transcendentals=0),
    )(asked)


def return_kernel(owners, back, owner, rank, out):
    capacity = back.shape[1]
    count = owner.shape[1]
    slot = lax.broadcasted_iota(jnp.int32, (capacity, count), 0) == rank[...]
    slot = jnp.where(slot, 1.0, 0.0).astype(BF16)
    picked = jnp.zeros((owners * ROWS, count), F32)
    for part in split3(back[...]):
        picked = picked + jnp.dot(part, slot, preferred_element_type=F32)
    target = owner[...]
    total = jnp.zeros((ROWS, count), F32)
    for o in range(owners):
        total = total + jnp.where(target == o, picked[o * ROWS : (o + 1) * ROWS], 0.0)
    out[...] = total[:6]


def returned(back, owner, rank, owners):
    count = owner.shape[1]

    def kernel(*refs):
        return_kernel(owners, *refs)

    return pl.pallas_call(
        kernel,
        out_shape=jax.ShapeDtypeStruct((6, count), F32),
        in_specs=[WHOLE] * 3,
        out_specs=WHOLE,
        compiler_params=PARAMS,
        cost_estimate=pl.CostEstimate(flops=6 * owners * ROWS * back.shape[1] * count, bytes_accessed=count * 100, transcendentals=0),
    )(back, owner, rank)


def y_band(size_y):
    radius = FW // 2
    place = np.concatenate([np.arange(size_y + radius), np.arange(-radius, 0)])
    offset = place[None, :] - np.arange(size_y)[:, None] + radius
    g = np.array(taps())
    return np.where((offset >= 0) & (offset <= FW), g[np.clip(offset, 0, FW)], 0.0).astype(np.float32)


def y_strips(edges):
    radius = FW // 2
    devices = lax.axis_size("gy")
    if devices == 2:
        return lax.ppermute(edges, "gy", [(0, 1), (1, 0)])
    up = [(i, (i + 1) % devices) for i in range(devices)]
    down = [(j, i) for i, j in up]
    after = lax.ppermute(edges[..., :radius], "gy", down)
    before = lax.ppermute(edges[..., radius:], "gy", up)
    return jnp.concatenate([after, before], axis=-1)


def on_device(velocity, owner, cell_x, cell_y, cell_z, query_weights):
    _, size_z, size_x, size_y = velocity.shape
    owners = lax.axis_size("gx") * lax.axis_size("gy")
    count = owner.shape[0]
    capacity = 4 * count // owners

    left, right = neighbours(velocity, "gx")
    own_halo = neighbours(velocity, "gz")

    target = owner.reshape(1, count)
    cells = jnp.stack([cell_z, cell_x, cell_y])
    sent, rank = route(target, cells, query_weights, owners, capacity)
    asked = lax.all_to_all(sent.reshape(owners, ROWS, capacity), ("gx", "gy"), split_axis=0, concat_axis=0, tiled=True)
    asked = asked.transpose(1, 0, 2).reshape(ROWS, owners * capacity)
    w_high, w_low, w_y = hats(asked, size_z, size_x, size_y)

    left_halo = neighbours(left, "gz")
    right_halo = neighbours(right, "gz")
    own_z = along_z(own_halo[0], velocity, own_halo[1])
    left_z = along_z(left_halo[0], left, left_halo[1])
    right_z = along_z(right_halo[0], right, right_halo[1])
    fields, edges = along_x(left_z, own_z, right_z)
    values = samples(fields, y_strips(edges), jnp.asarray(y_band(size_y)), w_high, w_low, w_y)
    values = values.reshape(ROWS, owners, capacity).transpose(1, 0, 2)
    back = lax.all_to_all(values, ("gx", "gy"), split_axis=0, concat_axis=0, tiled=True)
    return returned(back.reshape(owners * ROWS, capacity), target, rank, owners)


def solution(mesh):
    placed = (
        P(None, "gz", "gx", "gy"),
        P(("gx", "gy", "gz"), None),
        P(("gx", "gy", "gz")),
        P(("gx", "gy", "gz")),
        P(("gx", "gy", "gz")),
        P(None, ("gx", "gy", "gz")),
    )
    return jax.shard_map(
        on_device,
        mesh=mesh,
        in_specs=placed,
        out_specs=P(None, ("gx", "gy", "gz")),
        check_vma=False,
    )
```

```python
import math

import jax
import jax.numpy as jnp
import numpy as np
from jax import lax
from jax.experimental import pallas as pl
from jax.experimental.pallas import tpu as pltpu
from jax.sharding import PartitionSpec as P

FW = 32
PAIRS = ((0, 0), (0, 1), (0, 2), (1, 1), (1, 2), (2, 2))
ROWS = 8
BLOCK = 256
F32 = jnp.float32
BF16 = jnp.bfloat16
WHOLE = pl.BlockSpec(memory_space=pltpu.VMEM)
PARAMS = pltpu.CompilerParams(vmem_limit_bytes=24 * 1024 * 1024)


def taps():
    radius = FW // 2
    values = [math.exp(-6.0 * (m - radius) ** 2 / FW**2) for m in range(2 * radius + 1)]
    return [v / sum(values) for v in values]


def neighbours(x, axis):
    devices = lax.axis_size(axis)
    up = [(i, (i + 1) % devices) for i in range(devices)]
    down = [(j, i) for i, j in up]
    return lax.ppermute(x, axis, up), lax.ppermute(x, axis, down)


def symmetric(values, centre):
    radius = FW // 2
    g = taps()
    totals = [g[radius] * values[centre]]
    for m in range(1, radius + 1):
        term = g[radius + m] * (values[centre - m] + values[centre + m])
        if m < 4:
            totals.append(term)
        else:
            totals[m % 4] = totals[m % 4] + term
    return (totals[0] + totals[1]) + (totals[2] + totals[3])


def split2(x):
    high = x.astype(BF16)
    return high, (x - high.astype(F32)).astype(BF16)


def split3(x):
    high, rest = x.astype(BF16), None
    rest = x - high.astype(F32)
    middle = rest.astype(BF16)
    return high, middle, (rest - middle.astype(F32)).astype(BF16)


def z_kernel(before, own, after, out, wide):
    layers, size_x = own.shape[1], own.shape[2]
    radius = FW // 2

    for part, (ref, skip) in enumerate(((before, layers - radius), (own, 0), (after, 0))):
        place = (0, radius, radius + layers)[part]

        def products(z, carry, ref=ref, skip=skip, place=place):
            u = [ref[k, z + skip] for k in range(3)]
            for k in range(3):
                wide[k, z + place] = u[k]
            for k, (a, b) in enumerate(PAIRS):
                wide[3 + k, z + place] = u[a] * u[b]
            return carry

        lax.fori_loop(0, layers if part == 1 else radius, products, 0)

    def filtered(f, carry):
        for x in range(0, size_x, 8):
            values = [wide[f, z, x : x + 8] for z in range(layers + 2 * radius)]
            for z in range(layers):
                out[f, z, x : x + 8] = symmetric(values, z + radius)
        return carry

    lax.fori_loop(0, 9, filtered, 0)


def along_z(before, own, after):
    _, z, x, y = own.shape
    return pl.pallas_call(
        z_kernel,
        out_shape=jax.ShapeDtypeStruct((9, z, x, y), F32),
        in_specs=[WHOLE] * 3,
        out_specs=WHOLE,
        scratch_shapes=[pltpu.VMEM((9, z + FW, x, y), F32)],
        compiler_params=PARAMS,
        cost_estimate=pl.CostEstimate(flops=9 * z * x * y * 66, bytes_accessed=21 * z * x * y * 4, transcendentals=0),
    )(before, own, after)


def x_kernel(before, own, after, out, strips, wide):
    layers, size_x, size_y = own.shape[1:]
    radius = FW // 2
    rows = layers * size_x

    def filtered(f, carry):
        for z in range(layers):
            wide[z, 0:radius] = before[f, z, size_x - radius :]
            wide[z, radius : radius + size_x] = own[f, z]
            wide[z, radius + size_x :] = after[f, z, :radius]
        for z in range(layers):
            values = [wide[z, i : i + 8] for i in range(size_x + FW - 7)]
            for x in range(0, size_x, 8):
                out[f, z * size_x + x : z * size_x + x + 8] = symmetric(values, x + radius)
        for n in range(0, rows, 128):
            turned = out[f, n : n + 128].T
            strips[f, :radius, n : n + 128] = turned[:radius]
            strips[f, radius:, n : n + 128] = turned[size_y - radius :]
        return carry

    lax.fori_loop(0, 9, filtered, 0)


def along_x(before, own, after):
    _, z, x, y = own.shape
    return pl.pallas_call(
        x_kernel,
        out_shape=(
            jax.ShapeDtypeStruct((9, z * x, y), F32),
            jax.ShapeDtypeStruct((9, FW, z * x), F32),
        ),
        in_specs=[WHOLE] * 3,
        out_specs=(WHOLE, WHOLE),
        scratch_shapes=[pltpu.VMEM((z, x + FW, y), F32)],
        compiler_params=PARAMS,
        cost_estimate=pl.CostEstimate(flops=9 * z * x * y * 66, bytes_accessed=40 * z * x * y * 4, transcendentals=0),
    )(before, own, after)


def y_kernel(band, fields, asked, out, busy):
    def filtered(f, carry):
        out[f] = lax.dot_general(
            band[...], fields[f], (((1,), (1,)), ((), ())),
            precision=lax.Precision.HIGHEST, preferred_element_type=F32,
        )
        return carry

    lax.fori_loop(0, 9, filtered, 0)
    groups, _, capacity = asked.shape
    for n in range(busy.shape[0]):
        group, start = divmod(n * BLOCK, capacity)
        busy[n] = jnp.max(asked[group, 0:1, start : start + BLOCK]).astype(jnp.int32)


def along_y(band, fields, asked):
    _, cells, size_y = fields.shape
    return pl.pallas_call(
        y_kernel,
        out_shape=(
            jax.ShapeDtypeStruct((9, size_y, cells), F32),
            jax.ShapeDtypeStruct((asked.shape[0] * asked.shape[2] // BLOCK,), jnp.int32),
        ),
        in_specs=[WHOLE] * 3,
        out_specs=(WHOLE, pl.BlockSpec(memory_space=pltpu.SMEM)),
        compiler_params=PARAMS,
        cost_estimate=pl.CostEstimate(flops=9 * 12 * size_y * size_y * cells, bytes_accessed=18 * cells * size_y * 4, transcendentals=0),
    )(band, fields, asked)


def hat(size, row, offset):
    distance = lax.broadcasted_iota(jnp.int32, (size, row.shape[1]), 0) - row
    return jnp.where(distance == 0, 1.0 - offset, jnp.where(distance == 1, offset, 0.0))


def sample_kernel(sizes, busy, partial, strips, band, asked, out, field_high, field_low):
    size_z, size_x, size_y = sizes
    capacity = asked.shape[2]

    def smooth(f):
        return partial[f] + jnp.dot(
            band[...], strips[f], precision=lax.Precision.HIGHEST, preferred_element_type=F32
        )

    mean = [smooth(k) for k in range(3)]
    for k, (a, b) in enumerate(PAIRS):
        high, low = split2(smooth(3 + k) - mean[a] * mean[b])
        field_high[k * size_y : (k + 1) * size_y] = high
        field_low[k * size_y : (k + 1) * size_y] = low

    blocks = capacity // BLOCK

    def sample(n, carry):
        group = n // blocks
        here = pl.ds(pl.multiple_of((n % blocks) * BLOCK, BLOCK), BLOCK)

        @pl.when(busy[n] == 0)
        def _():
            out[group, :, here] = jnp.zeros((ROWS, BLOCK), F32)

        @pl.when(busy[n] != 0)
        def _():
            cell = jnp.maximum(asked[group, 0:1, here].astype(jnp.int32) - 1, 0)
            wx, wy, wz = (asked[group, k : k + 1, here] for k in (1, 2, 3))
            in_z = hat(size_z, cell // (size_x * size_y), wz)
            in_x = hat(size_x, (cell // size_y) % size_x, wx)
            in_y = hat(size_y, cell % size_y, wy)
            high, low = split2(jnp.concatenate([in_z[z : z + 1] * in_x for z in range(size_z)], axis=0))
            wide = jnp.dot(field_high[...], high, preferred_element_type=F32)
            wide = wide + jnp.dot(field_low[...], high, preferred_element_type=F32)
            wide = wide + jnp.dot(field_high[...], low, preferred_element_type=F32)
            for k in range(6):
                part = wide[k * size_y : (k + 1) * size_y] * in_y
                out[group, k : k + 1, here] = jnp.sum(part, axis=0, keepdims=True)
            out[group, 6:ROWS, here] = jnp.zeros((ROWS - 6, BLOCK), F32)

        return carry

    lax.fori_loop(0, busy.shape[0], sample, 0)


def samples(busy, partial, strips, band, asked, sizes):
    _, size_y, cells = partial.shape
    groups, _, capacity = asked.shape

    def kernel(*refs):
        sample_kernel(sizes, *refs)

    return pl.pallas_call(
        kernel,
        out_shape=jax.ShapeDtypeStruct((groups, ROWS, capacity), F32),
        in_specs=[pl.BlockSpec(memory_space=pltpu.SMEM)] + [WHOLE] * 4,
        out_specs=WHOLE,
        scratch_shapes=[pltpu.VMEM((6 * size_y, cells), BF16), pltpu.VMEM((6 * size_y, cells), BF16)],
        compiler_params=PARAMS,
        cost_estimate=pl.CostEstimate(flops=6 * size_y * cells * groups * capacity * 6, bytes_accessed=8 * 1024 * 1024, transcendentals=0),
    )(busy, partial, strips, band, asked)


def route_kernel(sizes, owners, capacity, owner, cell_x, cell_y, cell_z, weights, out, rank_out):
    count = owner.shape[1]
    _, size_x, size_y = sizes
    target = owner[...]
    named = lax.broadcasted_iota(jnp.int32, (owners, count), 0) == target
    earlier = lax.broadcasted_iota(jnp.int32, (count, count), 0) < lax.broadcasted_iota(jnp.int32, (count, count), 1)
    before = jnp.dot(
        jnp.where(named, 1.0, 0.0).astype(BF16), jnp.where(earlier, 1.0, 0.0).astype(BF16),
        preferred_element_type=F32,
    )
    rank = jnp.sum(jnp.where(named, before, 0.0), axis=0, keepdims=True).astype(jnp.int32)
    rank_out[...] = rank
    slot = lax.broadcasted_iota(jnp.int32, (capacity, count), 0) == rank
    slot = jnp.where(slot, 1.0, 0.0).astype(BF16)
    cell = (cell_z[...] * size_x + cell_x[...]) * size_y + cell_y[...] + 1
    record = jnp.concatenate([cell.astype(F32), weights[...], jnp.zeros((4, count), F32)], axis=0)
    total = jnp.zeros((owners * 8, capacity), F32)
    for part in split3(record):
        part = part.astype(F32)
        spread = jnp.concatenate(
            [jnp.where(target == o, part, 0.0) for o in range(owners)], axis=0
        ).astype(BF16)
        total = total + lax.dot_general(spread, slot, (((1,), (1,)), ((), ())), preferred_element_type=F32)
    for o in range(owners):
        out[o] = total[o * 8 : o * 8 + 4]


def route(owner, cell_x, cell_y, cell_z, weights, sizes, owners, capacity):
    count = owner.shape[1]

    def kernel(*refs):
        route_kernel(sizes, owners, capacity, *refs)

    return pl.pallas_call(
        kernel,
        out_shape=(
            jax.ShapeDtypeStruct((owners, 4, capacity), F32),
            jax.ShapeDtypeStruct((1, count), jnp.int32),
        ),
        in_specs=[WHOLE] * 5,
        out_specs=(WHOLE, WHOLE),
        compiler_params=PARAMS,
        cost_estimate=pl.CostEstimate(flops=10 * count * count * owners, bytes_accessed=count * 4 * 40, transcendentals=0),
    )(owner, cell_x, cell_y, cell_z, weights)


def return_kernel(owners, back, owner, rank, out):
    capacity = back.shape[1]
    count = owner.shape[1]
    slot = lax.broadcasted_iota(jnp.int32, (capacity, count), 0) == rank[...]
    slot = jnp.where(slot, 1.0, 0.0).astype(BF16)
    picked = jnp.zeros((owners * ROWS, count), F32)
    for part in split3(back[...]):
        picked = picked + jnp.dot(part, slot, preferred_element_type=F32)
    target = owner[...]
    total = jnp.zeros((ROWS, count), F32)
    for o in range(owners):
        total = total + jnp.where(target == o, picked[o * ROWS : (o + 1) * ROWS], 0.0)
    out[...] = total[:6]


def returned(back, owner, rank, owners):
    count = owner.shape[1]

    def kernel(*refs):
        return_kernel(owners, *refs)

    return pl.pallas_call(
        kernel,
        out_shape=jax.ShapeDtypeStruct((6, count), F32),
        in_specs=[WHOLE] * 3,
        out_specs=WHOLE,
        compiler_params=PARAMS,
        cost_estimate=pl.CostEstimate(flops=6 * owners * ROWS * back.shape[1] * count, bytes_accessed=count * 100, transcendentals=0),
    )(back, owner, rank)


def y_band(size_y):
    radius = FW // 2
    place = np.concatenate([np.arange(size_y + radius), np.arange(-radius, 0)])
    offset = place[None, :] - np.arange(size_y)[:, None] + radius
    g = np.array(taps())
    band = np.where((offset >= 0) & (offset <= FW), g[np.clip(offset, 0, FW)], 0.0)
    return band[:, :size_y].astype(np.float32), band[:, size_y:].astype(np.float32)


def y_strips(edges):
    radius = FW // 2
    devices = lax.axis_size("gy")
    if devices == 2:
        return lax.ppermute(edges, "gy", [(0, 1), (1, 0)])
    up = [(i, (i + 1) % devices) for i in range(devices)]
    down = [(j, i) for i, j in up]
    after = lax.ppermute(edges[:, :radius], "gy", down)
    before = lax.ppermute(edges[:, radius:], "gy", up)
    return jnp.concatenate([after, before], axis=1)


def on_device(velocity, owner, cell_x, cell_y, cell_z, query_weights):
    _, size_z, size_x, size_y = velocity.shape
    owners = lax.axis_size("gx") * lax.axis_size("gy")
    count = owner.shape[0]
    capacity = 4 * count // owners

    sizes = (size_z, size_x, size_y)
    folded = capacity % BLOCK != 0

    left, right = neighbours(velocity, "gx")
    own_halo = neighbours(velocity, "gz")

    target = owner.reshape(1, count)
    sent, rank = route(
        target, cell_x.reshape(1, count), cell_y.reshape(1, count), cell_z.reshape(1, count), query_weights,
        sizes, owners, capacity,
    )
    asked = lax.all_to_all(sent, ("gx", "gy"), split_axis=0, concat_axis=0, tiled=True)
    left, asked = lax.optimization_barrier((left, asked))
    if folded:
        asked = asked.transpose(1, 0, 2).reshape(1, 4, owners * capacity)

    left_halo = neighbours(left, "gz")
    right_halo = neighbours(right, "gz")
    own_z = along_z(own_halo[0], velocity, own_halo[1])
    left_z = along_z(left_halo[0], left, left_halo[1])
    right_z = along_z(right_halo[0], right, right_halo[1])
    fields, edges = along_x(left_z, own_z, right_z)
    band_own, band_strips = y_band(size_y)
    strips = y_strips(edges)
    partial, busy = along_y(jnp.asarray(band_own), fields, asked)
    values = samples(busy, partial, strips, jnp.asarray(band_strips), asked, sizes)
    if folded:
        values = values.reshape(ROWS, owners, capacity).transpose(1, 0, 2)
    back = lax.all_to_all(values, ("gx", "gy"), split_axis=0, concat_axis=0, tiled=True)
    return returned(back.reshape(owners * ROWS, capacity), target, rank, owners)


def solution(mesh):
    placed = (
        P(None, "gz", "gx", "gy"),
        P(("gx", "gy", "gz"), None),
        P(("gx", "gy", "gz")),
        P(("gx", "gy", "gz")),
        P(("gx", "gy", "gz")),
        P(None, ("gx", "gy", "gz")),
    )
    return jax.shard_map(
        on_device,
        mesh=mesh,
        in_specs=placed,
        out_specs=P(None, ("gx", "gy", "gz")),
        check_vma=False,
    )
```

```python
import math

import jax
import jax.numpy as jnp
import numpy as np
from jax import lax
from jax.experimental import pallas as pl
from jax.experimental.pallas import tpu as pltpu
from jax.sharding import PartitionSpec as P

FW = 32
PAIRS = ((0, 0), (0, 1), (0, 2), (1, 1), (1, 2), (2, 2))
ROWS = 8
BLOCK = 256
F32 = jnp.float32
BF16 = jnp.bfloat16
WHOLE = pl.BlockSpec(memory_space=pltpu.VMEM)
PARAMS = pltpu.CompilerParams(vmem_limit_bytes=24 * 1024 * 1024)


def taps():
    radius = FW // 2
    values = [math.exp(-6.0 * (m - radius) ** 2 / FW**2) for m in range(2 * radius + 1)]
    return [v / sum(values) for v in values]


def shifted(x, axis, step):
    devices = lax.axis_size(axis)
    return lax.ppermute(x, axis, [(i, (i + step) % devices) for i in range(devices)])


def neighbours(x, axis):
    return shifted(x, axis, 1), shifted(x, axis, -1)


def after(x, *others):
    return lax.optimization_barrier((x, others))[0]


def relayed(brick):
    previous, following = neighbours(brick, "gz")
    return previous, brick, following


def symmetric(values, centre):
    radius = FW // 2
    g = taps()
    totals = [g[radius] * values[centre]]
    for m in range(1, radius + 1):
        term = g[radius + m] * (values[centre - m] + values[centre + m])
        if m < 4:
            totals.append(term)
        else:
            totals[m % 4] = totals[m % 4] + term
    return (totals[0] + totals[1]) + (totals[2] + totals[3])


def split2(x):
    high = x.astype(BF16)
    return high, (x - high.astype(F32)).astype(BF16)


def split3(x):
    high, rest = x.astype(BF16), None
    rest = x - high.astype(F32)
    middle = rest.astype(BF16)
    return high, middle, (rest - middle.astype(F32)).astype(BF16)


def form_products(before, own, after, wide):
    layers = own.shape[1]
    radius = FW // 2
    for part, (ref, skip) in enumerate(((before, layers - radius), (own, 0), (after, 0))):
        place = (0, radius, radius + layers)[part]

        def products(z, carry, ref=ref, skip=skip, place=place):
            u = [ref[k, z + skip] for k in range(3)]
            for k in range(3):
                wide[k, z + place] = u[k]
            for k, (a, b) in enumerate(PAIRS):
                wide[3 + k, z + place] = u[a] * u[b]
            return carry

        lax.fori_loop(0, layers if part == 1 else radius, products, 0, unroll=4)


def z_kernel(before, own, after, out, wide):
    layers, size_x = own.shape[1], own.shape[2]
    radius = FW // 2
    form_products(before, own, after, wide)

    def filtered(f, carry):
        for x in range(0, size_x, 8):
            values = [wide[f, z, x : x + 8] for z in range(layers + 2 * radius)]
            for z in range(layers):
                out[f, z, x : x + 8] = symmetric(values, z + radius)
        return carry

    lax.fori_loop(0, 9, filtered, 0)


def along_z(before, own, after):
    _, z, x, y = own.shape
    return pl.pallas_call(
        z_kernel,
        out_shape=jax.ShapeDtypeStruct((9, z, x, y), F32),
        in_specs=[WHOLE] * 3,
        out_specs=WHOLE,
        scratch_shapes=[pltpu.VMEM((9, z + FW, x, y), F32)],
        compiler_params=PARAMS,
        cost_estimate=pl.CostEstimate(flops=9 * z * x * y * 66, bytes_accessed=21 * z * x * y * 4, transcendentals=0),
    )(before, own, after)


def near_kernel(before, own, after, out, wide):
    layers, size_x = own.shape[1:3]
    half = before.shape[2]
    empty = jnp.zeros((size_x - half, own.shape[3]), F32)
    for z in range(layers):
        wide[z, : size_x - half] = empty
        wide[z, 2 * size_x + half :] = empty

    def filtered(f, carry):
        for z in range(layers):
            wide[z, size_x - half : size_x] = before[f, z]
            wide[z, size_x : 2 * size_x] = own[f, z]
            wide[z, 2 * size_x : 2 * size_x + half] = after[f, z]
        for z in range(layers):
            values = [wide[z, i : i + 8] for i in range(3 * size_x - 7)]
            for x in range(0, size_x, 8):
                out[f, z * size_x + x : z * size_x + x + 8] = symmetric(values, x + size_x)
        return carry

    lax.fori_loop(0, 9, filtered, 0)


def along_x_near(before, own, after):
    _, z, x, y = own.shape
    return pl.pallas_call(
        near_kernel,
        out_shape=jax.ShapeDtypeStruct((9, z * x, y), F32),
        in_specs=[WHOLE] * 3,
        out_specs=WHOLE,
        scratch_shapes=[pltpu.VMEM((z, 3 * x, y), F32)],
        compiler_params=PARAMS,
        cost_estimate=pl.CostEstimate(flops=9 * z * x * y * 66, bytes_accessed=30 * z * x * y * 4, transcendentals=0),
    )(before, own, after)


def far_kernel(leading, last, before, own, after, near, out, *rest):
    strips = rest[0] if last else None
    wide, padded = rest[-2:]
    layers, half, size_y = own.shape[1:]
    radius = FW // 2
    size_x = near.shape[1] // layers
    g = taps()
    form_products(before, own, after, wide)
    empty = jnp.zeros((half, size_y), F32)
    for z in range(layers):
        if leading:
            padded[z, half:] = empty
        else:
            padded[z, :half] = empty

    def filtered(f, carry):
        values = [wide[f, z] for z in range(layers + 2 * radius)]
        for z in range(layers):
            if leading:
                padded[z, :half] = symmetric(values, z + radius)
            else:
                padded[z, half:] = symmetric(values, z + radius)
        for z in range(layers):
            start = z * size_x
            if leading:
                added = [g[k] * padded[z, k : k + half] for k in range(half)]
            else:
                added = [g[2 * radius - k] * padded[z, half - k : 2 * half - k] for k in range(half)]
                start = start + half
            while len(added) > 1:
                added = [p + q for p, q in zip(added[::2], added[1::2])] + added[len(added) // 2 * 2 :]
            other = z * size_x + (half if leading else 0)
            out[f, start : start + half] = near[f, start : start + half] + added[0]
            out[f, other : other + half] = near[f, other : other + half]
        if last:
            for n in range(0, layers * size_x, 128):
                turned = out[f, n : n + 128].T
                strips[f, :radius, n : n + 128] = turned[:radius]
                strips[f, radius:, n : n + 128] = turned[size_y - radius :]
        return carry

    lax.fori_loop(0, 9, filtered, 0)


def along_x_far(leading, last, before, own, after, near):
    _, z, half, y = own.shape
    cells = near.shape[1]

    def kernel(*refs):
        far_kernel(leading, last, *refs)

    out_shape = jax.ShapeDtypeStruct((9, cells, y), F32)
    out_spec = WHOLE
    if last:
        out_shape = (out_shape, jax.ShapeDtypeStruct((9, FW, cells), F32))
        out_spec = (WHOLE, WHOLE)
    return pl.pallas_call(
        kernel,
        out_shape=out_shape,
        in_specs=[WHOLE] * 4,
        out_specs=out_spec,
        scratch_shapes=[pltpu.VMEM((9, z + FW, half, y), F32), pltpu.VMEM((z, 2 * half, y), F32)],
        compiler_params=PARAMS,
        cost_estimate=pl.CostEstimate(flops=9 * z * half * y * 90, bytes_accessed=40 * z * half * y * 4, transcendentals=0),
    )(before, own, after, near)


def hat(size, row, offset):
    distance = lax.broadcasted_iota(jnp.int32, (size, row.shape[1]), 0) - row
    return jnp.where(distance == 0, 1.0 - offset, jnp.where(distance == 1, offset, 0.0))


def y_kernel(sizes, band, fields, asked, out, w_high, w_low, w_y):
    size_z, size_x, size_y = sizes

    def filtered(f, carry):
        out[f] = lax.dot_general(
            band[...], fields[f], (((1,), (1,)), ((), ())),
            precision=lax.Precision.HIGHEST, preferred_element_type=F32,
        )
        return carry

    lax.fori_loop(0, 9, filtered, 0)
    blocks = asked.shape[2] // BLOCK

    def weights(n, carry):
        group = n // blocks
        here = pl.ds(pl.multiple_of((n % blocks) * BLOCK, BLOCK), BLOCK)
        there = pl.ds(pl.multiple_of(n * BLOCK, BLOCK), BLOCK)
        cell = asked[group, 0:1, here].astype(jnp.int32)
        wx, wy, wz = (asked[group, k : k + 1, here] for k in (1, 2, 3))
        in_z = hat(size_z, cell // (size_x * size_y), wz)
        in_x = hat(size_x, (cell // size_y) % size_x, wx)
        w_y[:, there] = hat(size_y, cell % size_y, wy)
        for z in range(size_z):
            high, low = split2(in_z[z : z + 1] * in_x)
            w_high[z * size_x : (z + 1) * size_x, there] = high
            w_low[z * size_x : (z + 1) * size_x, there] = low
        return carry

    lax.fori_loop(0, asked.shape[0] * blocks, weights, 0)


def along_y(band, fields, asked, sizes):
    _, cells, size_y = fields.shape
    count = asked.shape[0] * asked.shape[2]

    def kernel(*refs):
        y_kernel(sizes, *refs)

    return pl.pallas_call(
        kernel,
        out_shape=(
            jax.ShapeDtypeStruct((9, size_y, cells), F32),
            jax.ShapeDtypeStruct((cells, count), BF16),
            jax.ShapeDtypeStruct((cells, count), BF16),
            jax.ShapeDtypeStruct((size_y, count), F32),
        ),
        in_specs=[WHOLE] * 3,
        out_specs=(WHOLE,) * 4,
        compiler_params=PARAMS,
        cost_estimate=pl.CostEstimate(flops=9 * 12 * size_y * size_y * cells, bytes_accessed=18 * cells * size_y * 4, transcendentals=0),
    )(band, fields, asked)


def sample_kernel(partial, strips, band, w_high, w_low, w_y, out, field_high, field_low):
    size_y = partial.shape[1]
    blocks = out.shape[2] // BLOCK

    def smooth(f):
        return partial[f] + jnp.dot(
            band[...], strips[f], precision=lax.Precision.HIGHEST, preferred_element_type=F32
        )

    mean = [smooth(k) for k in range(3)]
    for k, (a, b) in enumerate(PAIRS):
        high, low = split2(smooth(3 + k) - mean[a] * mean[b])
        field_high[k * size_y : (k + 1) * size_y] = high
        field_low[k * size_y : (k + 1) * size_y] = low

    def sample(n, carry):
        group = n // blocks
        here = pl.ds(pl.multiple_of((n % blocks) * BLOCK, BLOCK), BLOCK)
        there = pl.ds(pl.multiple_of(n * BLOCK, BLOCK), BLOCK)
        high = w_high[:, there]
        wide = jnp.dot(field_high[...], high, preferred_element_type=F32)
        wide = wide + jnp.dot(field_low[...], high, preferred_element_type=F32)
        wide = wide + jnp.dot(field_high[...], w_low[:, there], preferred_element_type=F32)
        in_y = w_y[:, there]
        for k in range(6):
            part = wide[k * size_y : (k + 1) * size_y] * in_y
            out[group, k : k + 1, here] = jnp.sum(part, axis=0, keepdims=True)
        out[group, 6:ROWS, here] = jnp.zeros((ROWS - 6, BLOCK), F32)
        return carry

    lax.fori_loop(0, out.shape[0] * blocks, sample, 0, unroll=4)


def samples(partial, strips, band, w_high, w_low, w_y, groups):
    _, size_y, cells = partial.shape
    count = w_y.shape[1]
    return pl.pallas_call(
        sample_kernel,
        out_shape=jax.ShapeDtypeStruct((groups, ROWS, count // groups), F32),
        in_specs=[WHOLE] * 6,
        out_specs=WHOLE,
        scratch_shapes=[pltpu.VMEM((6 * size_y, cells), BF16), pltpu.VMEM((6 * size_y, cells), BF16)],
        compiler_params=PARAMS,
        cost_estimate=pl.CostEstimate(flops=6 * size_y * cells * count * 6, bytes_accessed=8 * 1024 * 1024, transcendentals=0),
    )(partial, strips, band, w_high, w_low, w_y)


def route_kernel(owners, capacity, record, owner, out, rank_out):
    count = record.shape[1]
    target = owner[...]
    named = lax.broadcasted_iota(jnp.int32, (owners, count), 0) == target
    earlier = lax.broadcasted_iota(jnp.int32, (count, count), 0) < lax.broadcasted_iota(jnp.int32, (count, count), 1)
    before = jnp.dot(
        jnp.where(named, 1.0, 0.0).astype(BF16), jnp.where(earlier, 1.0, 0.0).astype(BF16),
        preferred_element_type=F32,
    )
    rank = jnp.sum(jnp.where(named, before, 0.0), axis=0, keepdims=True).astype(jnp.int32)
    rank_out[...] = rank
    slot = lax.broadcasted_iota(jnp.int32, (capacity, count), 0) == rank
    slot = jnp.where(slot, 1.0, 0.0).astype(BF16)
    values = jnp.concatenate([record[...], jnp.zeros((4, count), F32)], axis=0)
    total = jnp.zeros((owners * 8, capacity), F32)
    for part in split3(values):
        part = part.astype(F32)
        spread = jnp.concatenate(
            [jnp.where(target == o, part, 0.0) for o in range(owners)], axis=0
        ).astype(BF16)
        total = total + lax.dot_general(spread, slot, (((1,), (1,)), ((), ())), preferred_element_type=F32)
    for o in range(owners):
        out[o] = total[o * 8 : o * 8 + 4]


def route(record, owner, owners, capacity):
    count = record.shape[1]

    def kernel(*refs):
        route_kernel(owners, capacity, *refs)

    return pl.pallas_call(
        kernel,
        out_shape=(
            jax.ShapeDtypeStruct((owners, 4, capacity), F32),
            jax.ShapeDtypeStruct((1, count), jnp.int32),
        ),
        in_specs=[WHOLE] * 2,
        out_specs=(WHOLE, WHOLE),
        compiler_params=PARAMS,
        cost_estimate=pl.CostEstimate(flops=10 * count * count * owners, bytes_accessed=count * 4 * 40, transcendentals=0),
    )(record, owner)


def return_kernel(owners, back, owner, rank, out):
    capacity = back.shape[1]
    count = owner.shape[1]
    slot = lax.broadcasted_iota(jnp.int32, (capacity, count), 0) == rank[...]
    slot = jnp.where(slot, 1.0, 0.0).astype(BF16)
    picked = jnp.zeros((owners * ROWS, count), F32)
    for part in split3(back[...]):
        picked = picked + jnp.dot(part, slot, preferred_element_type=F32)
    target = owner[...]
    total = jnp.zeros((ROWS, count), F32)
    for o in range(owners):
        total = total + jnp.where(target == o, picked[o * ROWS : (o + 1) * ROWS], 0.0)
    out[...] = total[:6]


def returned(back, owner, rank, owners):
    count = owner.shape[1]

    def kernel(*refs):
        return_kernel(owners, *refs)

    return pl.pallas_call(
        kernel,
        out_shape=jax.ShapeDtypeStruct((6, count), F32),
        in_specs=[WHOLE] * 3,
        out_specs=WHOLE,
        compiler_params=PARAMS,
        cost_estimate=pl.CostEstimate(flops=6 * owners * ROWS * back.shape[1] * count, bytes_accessed=count * 100, transcendentals=0),
    )(back, owner, rank)


def y_band(size_y):
    radius = FW // 2
    place = np.concatenate([np.arange(size_y + radius), np.arange(-radius, 0)])
    offset = place[None, :] - np.arange(size_y)[:, None] + radius
    g = np.array(taps())
    band = np.where((offset >= 0) & (offset <= FW), g[np.clip(offset, 0, FW)], 0.0)
    return band[:, :size_y].astype(np.float32), band[:, size_y:].astype(np.float32)


def y_strips(edges):
    radius = FW // 2
    devices = lax.axis_size("gy")
    if devices == 2:
        return lax.ppermute(edges, "gy", [(0, 1), (1, 0)])
    following = shifted(edges[:, :radius], "gy", -1)
    previous = shifted(edges[:, radius:], "gy", 1)
    return jnp.concatenate([following, previous], axis=1)


def on_device(velocity, owner, cell_x, cell_y, cell_z, query_weights):
    _, size_z, size_x, size_y = velocity.shape
    owners = lax.axis_size("gx") * lax.axis_size("gy")
    count = owner.shape[0]
    capacity = 4 * count // owners

    sizes = (size_z, size_x, size_y)
    folded = capacity % BLOCK != 0

    sizes = (size_z, size_x, size_y)
    half = size_x // 2
    folded = capacity % BLOCK != 0

    head, tail = velocity[:, :, :half], velocity[:, :, half:]
    near_left, near_right = shifted(tail, "gx", 1), shifted(head, "gx", -1)
    own_halo = neighbours(velocity, "gz")
    far_left = shifted(after(head, near_left), "gx", 1)
    far_right = shifted(after(tail, near_right), "gx", -1)

    cell = (cell_z * size_x + cell_x) * size_y + cell_y
    record = jnp.concatenate([cell.astype(F32).reshape(1, count), query_weights], axis=0)
    target = owner.reshape(1, count)
    sent, rank = route(record, target, owners, capacity)
    asked = lax.all_to_all(sent, ("gx", "gy"), split_axis=0, concat_axis=0, tiled=True)

    near_left = relayed(after(near_left, own_halo, sent))
    near_right = relayed(near_right)
    far_left = relayed(after(far_left, asked))
    far_right = relayed(far_right)
    if folded:
        asked = asked.transpose(1, 0, 2).reshape(1, 4, owners * capacity)
    own_z = along_z(own_halo[0], velocity, own_halo[1])
    left_z = along_z(*near_left)
    right_z = along_z(*near_right)
    fields = along_x_near(left_z, own_z, right_z)
    fields = along_x_far(True, False, *far_left, fields)
    fields, edges = along_x_far(False, True, *far_right, fields)
    band_own, band_strips = y_band(size_y)
    strips = y_strips(edges)
    partial, *weights = along_y(jnp.asarray(band_own), fields, asked, sizes)
    values = samples(partial, strips, jnp.asarray(band_strips), *weights, asked.shape[0])
    if folded:
        values = values.reshape(ROWS, owners, capacity).transpose(1, 0, 2)
    back = lax.all_to_all(values, ("gx", "gy"), split_axis=0, concat_axis=0, tiled=True)
    return returned(back.reshape(owners * ROWS, capacity), target, rank, owners)


def solution(mesh):
    placed = (
        P(None, "gz", "gx", "gy"),
        P(("gx", "gy", "gz"), None),
        P(("gx", "gy", "gz")),
        P(("gx", "gy", "gz")),
        P(("gx", "gy", "gz")),
        P(None, ("gx", "gy", "gz")),
    )
    return jax.shard_map(
        on_device,
        mesh=mesh,
        in_specs=placed,
        out_specs=P(None, ("gx", "gy", "gz")),
        check_vma=False,
    )
```

```python
import math

import jax
import jax.numpy as jnp
import numpy as np
from jax import lax
from jax.experimental import pallas as pl
from jax.experimental.pallas import tpu as pltpu
from jax.sharding import PartitionSpec as P

FW = 32
PAIRS = ((0, 0), (0, 1), (0, 2), (1, 1), (1, 2), (2, 2))
ROWS = 8
BLOCK = 256
F32 = jnp.float32
BF16 = jnp.bfloat16
WHOLE = pl.BlockSpec(memory_space=pltpu.VMEM)
PARAMS = pltpu.CompilerParams(vmem_limit_bytes=24 * 1024 * 1024)


def taps():
    radius = FW // 2
    values = [math.exp(-6.0 * (m - radius) ** 2 / FW**2) for m in range(2 * radius + 1)]
    return [v / sum(values) for v in values]


def shifted(x, axis, step):
    devices = lax.axis_size(axis)
    return lax.ppermute(x, axis, [(i, (i + step) % devices) for i in range(devices)])


def neighbours(x, axis):
    return shifted(x, axis, 1), shifted(x, axis, -1)


def after(x, *others):
    return lax.optimization_barrier((x, others))[0]


def relayed(brick):
    previous, following = neighbours(brick, "gz")
    return previous, brick, following


def symmetric(values, centre):
    radius = FW // 2
    g = taps()
    totals = [g[radius] * values[centre]]
    for m in range(1, radius + 1):
        term = g[radius + m] * (values[centre - m] + values[centre + m])
        if m < 4:
            totals.append(term)
        else:
            totals[m % 4] = totals[m % 4] + term
    return (totals[0] + totals[1]) + (totals[2] + totals[3])


def split2(x):
    high = x.astype(BF16)
    return high, (x - high.astype(F32)).astype(BF16)


def split3(x):
    high, rest = x.astype(BF16), None
    rest = x - high.astype(F32)
    middle = rest.astype(BF16)
    return high, middle, (rest - middle.astype(F32)).astype(BF16)


def form_products(before, own, after, wide):
    layers = own.shape[1]
    radius = FW // 2
    for part, (ref, skip) in enumerate(((before, layers - radius), (own, 0), (after, 0))):
        place = (0, radius, radius + layers)[part]

        def products(z, carry, ref=ref, skip=skip, place=place):
            u = [ref[k, z + skip] for k in range(3)]
            for k in range(3):
                wide[k, z + place] = u[k]
            for k, (a, b) in enumerate(PAIRS):
                wide[3 + k, z + place] = u[a] * u[b]
            return carry

        lax.fori_loop(0, layers if part == 1 else radius, products, 0, unroll=4)


def z_kernel(before, own, after, out, wide):
    layers, size_x = own.shape[1], own.shape[2]
    radius = FW // 2
    form_products(before, own, after, wide)

    def filtered(f, carry):
        for x in range(0, size_x, 8):
            values = [wide[f, z, x : x + 8] for z in range(layers + 2 * radius)]
            for z in range(layers):
                out[f, z, x : x + 8] = symmetric(values, z + radius)
        return carry

    lax.fori_loop(0, 9, filtered, 0)


def along_z(before, own, after):
    _, z, x, y = own.shape
    return pl.pallas_call(
        z_kernel,
        out_shape=jax.ShapeDtypeStruct((9, z, x, y), F32),
        in_specs=[WHOLE] * 3,
        out_specs=WHOLE,
        scratch_shapes=[pltpu.VMEM((9, z + FW, x, y), F32)],
        compiler_params=PARAMS,
        cost_estimate=pl.CostEstimate(flops=9 * z * x * y * 66, bytes_accessed=21 * z * x * y * 4, transcendentals=0),
    )(before, own, after)


def first_kernel(own, right, out, wide):
    layers, size_x = own.shape[1:3]
    radius = FW // 2
    empty = jnp.zeros((radius, own.shape[3]), F32)
    for z in range(layers):
        wide[z, :radius] = empty

    def filtered(f, carry):
        for z in range(layers):
            wide[z, radius : radius + size_x] = own[f, z]
            wide[z, radius + size_x :] = right[f, z, :radius]
        for z in range(layers):
            values = [wide[z, i : i + 8] for i in range(size_x + FW - 7)]
            for x in range(0, size_x, 8):
                out[f, z * size_x + x : z * size_x + x + 8] = symmetric(values, x + radius)
        return carry

    lax.fori_loop(0, 9, filtered, 0)


def along_x_first(own, right):
    _, z, x, y = own.shape
    return pl.pallas_call(
        first_kernel,
        out_shape=jax.ShapeDtypeStruct((9, z * x, y), F32),
        in_specs=[WHOLE] * 2,
        out_specs=WHOLE,
        scratch_shapes=[pltpu.VMEM((z, x + FW, y), F32)],
        compiler_params=PARAMS,
        cost_estimate=pl.CostEstimate(flops=9 * z * x * y * 66, bytes_accessed=30 * z * x * y * 4, transcendentals=0),
    )(own, right)


def last_kernel(before, own, after, partial, out, strips, wide, padded):
    layers, size_x, size_y = own.shape[1:]
    radius = FW // 2
    g = taps()
    form_products(before, own, after, wide)
    empty = jnp.zeros((size_x, size_y), F32)
    for z in range(layers):
        padded[z, size_x:] = empty

    def filtered(f, carry):
        for x in range(0, size_x, 8):
            values = [wide[f, z, x : x + 8] for z in range(layers + 2 * radius)]
            for z in range(layers):
                padded[z, x : x + 8] = symmetric(values, z + radius)
        for z in range(layers):
            for x in range(0, size_x, 8):
                added = [
                    g[radius - size_x + k] * padded[z, x + k : x + k + 8]
                    for k in range(size_x - radius, size_x - x)
                ]
                while len(added) > 1:
                    added = [p + q for p, q in zip(added[::2], added[1::2])] + added[len(added) // 2 * 2 :]
                row = z * size_x + x
                out[f, row : row + 8] = partial[f, row : row + 8] + added[0]
        for n in range(0, layers * size_x, 128):
            turned = out[f, n : n + 128].T
            strips[f, :radius, n : n + 128] = turned[:radius]
            strips[f, radius:, n : n + 128] = turned[size_y - radius :]
        return carry

    lax.fori_loop(0, 9, filtered, 0)


def along_x_last(before, own, after, partial):
    _, z, x, y = own.shape
    return pl.pallas_call(
        last_kernel,
        out_shape=(
            jax.ShapeDtypeStruct((9, z * x, y), F32),
            jax.ShapeDtypeStruct((9, FW, z * x), F32),
        ),
        in_specs=[WHOLE] * 4,
        out_specs=(WHOLE, WHOLE),
        scratch_shapes=[pltpu.VMEM((9, z + FW, x, y), F32), pltpu.VMEM((z, 2 * x, y), F32)],
        compiler_params=PARAMS,
        cost_estimate=pl.CostEstimate(flops=9 * z * x * y * 100, bytes_accessed=40 * z * x * y * 4, transcendentals=0),
    )(before, own, after, partial)


def hat(size, row, offset):
    distance = lax.broadcasted_iota(jnp.int32, (size, row.shape[1]), 0) - row
    return jnp.where(distance == 0, 1.0 - offset, jnp.where(distance == 1, offset, 0.0))


def y_kernel(sizes, band, fields, asked, out, w_high, w_low, w_y):
    size_z, size_x, size_y = sizes

    def filtered(f, carry):
        out[f] = lax.dot_general(
            band[...], fields[f], (((1,), (1,)), ((), ())),
            precision=lax.Precision.HIGHEST, preferred_element_type=F32,
        )
        return carry

    lax.fori_loop(0, 9, filtered, 0)
    blocks = asked.shape[2] // BLOCK

    def weights(n, carry):
        group = n // blocks
        here = pl.ds(pl.multiple_of((n % blocks) * BLOCK, BLOCK), BLOCK)
        there = pl.ds(pl.multiple_of(n * BLOCK, BLOCK), BLOCK)
        cell = asked[group, 0:1, here].astype(jnp.int32)
        wx, wy, wz = (asked[group, k : k + 1, here] for k in (1, 2, 3))
        in_z = hat(size_z, cell // (size_x * size_y), wz)
        in_x = hat(size_x, (cell // size_y) % size_x, wx)
        w_y[:, there] = hat(size_y, cell % size_y, wy)
        for z in range(size_z):
            high, low = split2(in_z[z : z + 1] * in_x)
            w_high[z * size_x : (z + 1) * size_x, there] = high
            w_low[z * size_x : (z + 1) * size_x, there] = low
        return carry

    lax.fori_loop(0, asked.shape[0] * blocks, weights, 0)


def along_y(band, fields, asked, sizes):
    _, cells, size_y = fields.shape
    count = asked.shape[0] * asked.shape[2]

    def kernel(*refs):
        y_kernel(sizes, *refs)

    return pl.pallas_call(
        kernel,
        out_shape=(
            jax.ShapeDtypeStruct((9, size_y, cells), F32),
            jax.ShapeDtypeStruct((cells, count), BF16),
            jax.ShapeDtypeStruct((cells, count), BF16),
            jax.ShapeDtypeStruct((size_y, count), F32),
        ),
        in_specs=[WHOLE] * 3,
        out_specs=(WHOLE,) * 4,
        compiler_params=PARAMS,
        cost_estimate=pl.CostEstimate(flops=9 * 12 * size_y * size_y * cells, bytes_accessed=18 * cells * size_y * 4, transcendentals=0),
    )(band, fields, asked)


def sample_kernel(partial, strips, band, w_high, w_low, w_y, out, field_high, field_low):
    size_y = partial.shape[1]
    blocks = out.shape[2] // BLOCK

    def smooth(f):
        return partial[f] + jnp.dot(
            band[...], strips[f], precision=lax.Precision.HIGHEST, preferred_element_type=F32
        )

    mean = [smooth(k) for k in range(3)]
    for k, (a, b) in enumerate(PAIRS):
        high, low = split2(smooth(3 + k) - mean[a] * mean[b])
        field_high[k * size_y : (k + 1) * size_y] = high
        field_low[k * size_y : (k + 1) * size_y] = low

    def sample(n, carry):
        group = n // blocks
        here = pl.ds(pl.multiple_of((n % blocks) * BLOCK, BLOCK), BLOCK)
        there = pl.ds(pl.multiple_of(n * BLOCK, BLOCK), BLOCK)
        high = w_high[:, there]
        wide = jnp.dot(field_high[...], high, preferred_element_type=F32)
        wide = wide + jnp.dot(field_low[...], high, preferred_element_type=F32)
        wide = wide + jnp.dot(field_high[...], w_low[:, there], preferred_element_type=F32)
        in_y = w_y[:, there]
        for k in range(6):
            part = wide[k * size_y : (k + 1) * size_y] * in_y
            out[group, k : k + 1, here] = jnp.sum(part, axis=0, keepdims=True)
        out[group, 6:ROWS, here] = jnp.zeros((ROWS - 6, BLOCK), F32)
        return carry

    lax.fori_loop(0, out.shape[0] * blocks, sample, 0, unroll=4)


def samples(partial, strips, band, w_high, w_low, w_y, groups):
    _, size_y, cells = partial.shape
    count = w_y.shape[1]
    return pl.pallas_call(
        sample_kernel,
        out_shape=jax.ShapeDtypeStruct((groups, ROWS, count // groups), F32),
        in_specs=[WHOLE] * 6,
        out_specs=WHOLE,
        scratch_shapes=[pltpu.VMEM((6 * size_y, cells), BF16), pltpu.VMEM((6 * size_y, cells), BF16)],
        compiler_params=PARAMS,
        cost_estimate=pl.CostEstimate(flops=6 * size_y * cells * count * 6, bytes_accessed=8 * 1024 * 1024, transcendentals=0),
    )(partial, strips, band, w_high, w_low, w_y)


def route_kernel(owners, capacity, record, out, rank_out):
    count = record.shape[1]
    target = record[0:1].astype(jnp.int32)
    named = lax.broadcasted_iota(jnp.int32, (owners, count), 0) == target
    earlier = lax.broadcasted_iota(jnp.int32, (count, count), 0) < lax.broadcasted_iota(jnp.int32, (count, count), 1)
    before = jnp.dot(
        jnp.where(named, 1.0, 0.0).astype(BF16), jnp.where(earlier, 1.0, 0.0).astype(BF16),
        preferred_element_type=F32,
    )
    rank = jnp.sum(jnp.where(named, before, 0.0), axis=0, keepdims=True).astype(jnp.int32)
    rank_out[0:1] = rank
    rank_out[1:2] = target
    slot = lax.broadcasted_iota(jnp.int32, (capacity, count), 0) == rank
    slot = jnp.where(slot, 1.0, 0.0).astype(BF16)
    total = jnp.zeros((owners * 8, capacity), F32)
    for part in split3(record[...]):
        part = part.astype(F32)
        spread = jnp.concatenate(
            [jnp.where(target == o, part, 0.0) for o in range(owners)], axis=0
        ).astype(BF16)
        total = total + lax.dot_general(spread, slot, (((1,), (1,)), ((), ())), preferred_element_type=F32)
    for o in range(owners):
        out[o] = total[o * 8 + 1 : o * 8 + 5]


def route(record, owners, capacity):
    count = record.shape[1]

    def kernel(*refs):
        route_kernel(owners, capacity, *refs)

    return pl.pallas_call(
        kernel,
        out_shape=(
            jax.ShapeDtypeStruct((owners, 4, capacity), F32),
            jax.ShapeDtypeStruct((2, count), jnp.int32),
        ),
        in_specs=[WHOLE],
        out_specs=(WHOLE, WHOLE),
        compiler_params=PARAMS,
        cost_estimate=pl.CostEstimate(flops=10 * count * count * owners, bytes_accessed=count * 4 * 40, transcendentals=0),
    )(record)


def return_kernel(owners, back, place, out):
    capacity = back.shape[1]
    count = place.shape[1]
    slot = lax.broadcasted_iota(jnp.int32, (capacity, count), 0) == place[0:1]
    slot = jnp.where(slot, 1.0, 0.0).astype(BF16)
    picked = jnp.zeros((owners * ROWS, count), F32)
    for part in split3(back[...]):
        picked = picked + jnp.dot(part, slot, preferred_element_type=F32)
    target = place[1:2]
    total = jnp.zeros((ROWS, count), F32)
    for o in range(owners):
        total = total + jnp.where(target == o, picked[o * ROWS : (o + 1) * ROWS], 0.0)
    out[...] = total[:6]


def returned(back, place, owners):
    count = place.shape[1]

    def kernel(*refs):
        return_kernel(owners, *refs)

    return pl.pallas_call(
        kernel,
        out_shape=jax.ShapeDtypeStruct((6, count), F32),
        in_specs=[WHOLE] * 2,
        out_specs=WHOLE,
        compiler_params=PARAMS,
        cost_estimate=pl.CostEstimate(flops=6 * owners * ROWS * back.shape[1] * count, bytes_accessed=count * 100, transcendentals=0),
    )(back, place)


def y_band(size_y):
    radius = FW // 2
    place = np.concatenate([np.arange(size_y + radius), np.arange(-radius, 0)])
    offset = place[None, :] - np.arange(size_y)[:, None] + radius
    g = np.array(taps())
    band = np.where((offset >= 0) & (offset <= FW), g[np.clip(offset, 0, FW)], 0.0)
    return band[:, :size_y].astype(np.float32), band[:, size_y:].astype(np.float32)


def y_strips(edges):
    radius = FW // 2
    devices = lax.axis_size("gy")
    if devices == 2:
        return lax.ppermute(edges, "gy", [(0, 1), (1, 0)])
    following = shifted(edges[:, :radius], "gy", -1)
    previous = shifted(edges[:, radius:], "gy", 1)
    return jnp.concatenate([following, previous], axis=1)


def on_device(velocity, owner, cell_x, cell_y, cell_z, query_weights):
    _, size_z, size_x, size_y = velocity.shape
    owners = lax.axis_size("gx") * lax.axis_size("gy")
    count = owner.shape[0]
    capacity = 4 * count // owners

    sizes = (size_z, size_x, size_y)
    folded = capacity % BLOCK != 0

    sizes = (size_z, size_x, size_y)
    folded = capacity % BLOCK != 0

    row = lax.broadcasted_iota(jnp.int32, (8, count), 0)
    cell = (cell_z * size_x + cell_x) * size_y + cell_y
    record = jnp.pad(query_weights, ((2, 3), (0, 0)))
    record = jnp.where(row == 1, cell[None].astype(F32), record)
    record = jnp.where(row == 0, owner.reshape(1, count).astype(F32), record)
    sent, place = route(record, owners, capacity)

    asked = lax.all_to_all(sent, ("gx", "gy"), split_axis=0, concat_axis=0, tiled=True)

    right = shifted(velocity, "gx", -1)
    left = shifted(after(velocity, record), "gx", 1)
    own_halo = neighbours(velocity, "gz")
    right = relayed(right)
    left = relayed(after(left, asked))
    if folded:
        asked = asked.transpose(1, 0, 2).reshape(1, 4, owners * capacity)
    own_z = along_z(own_halo[0], velocity, own_halo[1])
    right_z = along_z(*right)
    fields, edges = along_x_last(*left, along_x_first(own_z, right_z))
    band_own, band_strips = y_band(size_y)
    strips = y_strips(edges)
    partial, *weights = along_y(jnp.asarray(band_own), fields, asked, sizes)
    values = samples(partial, strips, jnp.asarray(band_strips), *weights, asked.shape[0])
    if folded:
        values = values.reshape(ROWS, owners, capacity).transpose(1, 0, 2)
    back = lax.all_to_all(values, ("gx", "gy"), split_axis=0, concat_axis=0, tiled=True)
    return returned(back.reshape(owners * ROWS, capacity), place, owners)


def solution(mesh):
    placed = (
        P(None, "gz", "gx", "gy"),
        P(("gx", "gy", "gz"), None),
        P(("gx", "gy", "gz")),
        P(("gx", "gy", "gz")),
        P(("gx", "gy", "gz")),
        P(None, ("gx", "gy", "gz")),
    )
    return jax.shard_map(
        on_device,
        mesh=mesh,
        in_specs=placed,
        out_specs=P(None, ("gx", "gy", "gz")),
        check_vma=False,
    )
```

```python
import math

import jax
import jax.numpy as jnp
import numpy as np
from jax import lax
from jax.experimental import pallas as pl
from jax.experimental.pallas import tpu as pltpu
from jax.sharding import PartitionSpec as P

FW = 32
PAIRS = ((0, 0), (0, 1), (0, 2), (1, 1), (1, 2), (2, 2))
ROWS = 8
BLOCK = 256
F32 = jnp.float32
BF16 = jnp.bfloat16
WHOLE = pl.BlockSpec(memory_space=pltpu.VMEM)
PARAMS = pltpu.CompilerParams(vmem_limit_bytes=24 * 1024 * 1024)


def taps():
    radius = FW // 2
    values = [math.exp(-6.0 * (m - radius) ** 2 / FW**2) for m in range(2 * radius + 1)]
    return [v / sum(values) for v in values]


def shifted(x, axis, step):
    devices = lax.axis_size(axis)
    return lax.ppermute(x, axis, [(i, (i + step) % devices) for i in range(devices)])


def neighbours(x, axis):
    return shifted(x, axis, 1), shifted(x, axis, -1)


def after(x, *others):
    return lax.optimization_barrier((x, others))[0]


def relayed(brick):
    previous, following = neighbours(brick, "gz")
    return previous, brick, following


def symmetric(values, centre):
    radius = FW // 2
    g = taps()
    totals = [g[radius] * values[centre]]
    for m in range(1, radius + 1):
        term = g[radius + m] * (values[centre - m] + values[centre + m])
        if m < 4:
            totals.append(term)
        else:
            totals[m % 4] = totals[m % 4] + term
    return (totals[0] + totals[1]) + (totals[2] + totals[3])


def split2(x):
    high = x.astype(BF16)
    return high, (x - high.astype(F32)).astype(BF16)


def split3(x):
    high, rest = x.astype(BF16), None
    rest = x - high.astype(F32)
    middle = rest.astype(BF16)
    return high, middle, (rest - middle.astype(F32)).astype(BF16)


def form_products(before, own, after, wide, fields=tuple(range(9))):
    layers = own.shape[1]
    radius = FW // 2
    for part, (ref, skip) in enumerate(((before, layers - radius), (own, 0), (after, 0))):
        place = (0, radius, radius + layers)[part]

        def products(z, carry, ref=ref, skip=skip, place=place):
            u = [ref[k, z + skip] for k in range(3)]
            u = u + [u[a] * u[b] for a, b in PAIRS]
            for n, f in enumerate(fields):
                wide[n, z + place] = u[f]
            return carry

        lax.fori_loop(0, layers if part == 1 else radius, products, 0, unroll=4)


def z_kernel(before, own, after, out, wide):
    layers, size_x = own.shape[1], own.shape[2]
    radius = FW // 2
    form_products(before, own, after, wide)

    def filtered(f, carry):
        for x in range(0, size_x, 8):
            values = [wide[f, z, x : x + 8] for z in range(layers + 2 * radius)]
            for z in range(layers):
                out[f, z, x : x + 8] = symmetric(values, z + radius)
        return carry

    lax.fori_loop(0, 9, filtered, 0)


def along_z(before, own, after):
    _, z, x, y = own.shape
    return pl.pallas_call(
        z_kernel,
        out_shape=jax.ShapeDtypeStruct((9, z, x, y), F32),
        in_specs=[WHOLE] * 3,
        out_specs=WHOLE,
        scratch_shapes=[pltpu.VMEM((9, z + FW, x, y), F32)],
        compiler_params=PARAMS,
        cost_estimate=pl.CostEstimate(flops=9 * z * x * y * 66, bytes_accessed=21 * z * x * y * 4, transcendentals=0),
    )(before, own, after)


def first_kernel(own, right, out, wide):
    layers, size_x = own.shape[1:3]
    radius = FW // 2
    empty = jnp.zeros((radius, own.shape[3]), F32)
    for z in range(layers):
        wide[z, :radius] = empty

    def filtered(f, carry):
        for z in range(layers):
            wide[z, radius : radius + size_x] = own[f, z]
            wide[z, radius + size_x :] = right[f, z, :radius]
        for z in range(layers):
            values = [wide[z, i : i + 8] for i in range(size_x + FW - 7)]
            for x in range(0, size_x, 8):
                out[f, z * size_x + x : z * size_x + x + 8] = symmetric(values, x + radius)
        return carry

    lax.fori_loop(0, 9, filtered, 0)


def along_x_first(own, right):
    _, z, x, y = own.shape
    return pl.pallas_call(
        first_kernel,
        out_shape=jax.ShapeDtypeStruct((9, z * x, y), F32),
        in_specs=[WHOLE] * 2,
        out_specs=WHOLE,
        scratch_shapes=[pltpu.VMEM((z, x + FW, y), F32)],
        compiler_params=PARAMS,
        cost_estimate=pl.CostEstimate(flops=9 * z * x * y * 66, bytes_accessed=30 * z * x * y * 4, transcendentals=0),
    )(own, right)


def last_kernel(fields, before, own, after, partial, out, strips, wide, padded):
    layers, size_x, size_y = own.shape[1:]
    radius = FW // 2
    g = taps()
    form_products(before, own, after, wide, fields)
    empty = jnp.zeros((size_x, size_y), F32)
    for z in range(layers):
        padded[z, size_x:] = empty

    def filtered(f, carry):
        for x in range(0, size_x, 8):
            values = [wide[f, z, x : x + 8] for z in range(layers + 2 * radius)]
            for z in range(layers):
                padded[z, x : x + 8] = symmetric(values, z + radius)
        for z in range(layers):
            for x in range(0, size_x, 8):
                added = [
                    g[radius - size_x + k] * padded[z, x + k : x + k + 8]
                    for k in range(size_x - radius, size_x - x)
                ]
                while len(added) > 1:
                    added = [p + q for p, q in zip(added[::2], added[1::2])] + added[len(added) // 2 * 2 :]
                row = z * size_x + x
                out[f, row : row + 8] = partial[fields[0] + f, row : row + 8] + added[0]
        for n in range(0, layers * size_x, 128):
            turned = out[f, n : n + 128].T
            strips[f, :radius, n : n + 128] = turned[:radius]
            strips[f, radius:, n : n + 128] = turned[size_y - radius :]
        return carry

    lax.fori_loop(0, len(fields), filtered, 0)


def along_x_last(fields, before, own, after, partial):
    _, z, x, y = own.shape
    count = len(fields)

    def kernel(*refs):
        last_kernel(fields, *refs)

    return pl.pallas_call(
        kernel,
        out_shape=(
            jax.ShapeDtypeStruct((count, z * x, y), F32),
            jax.ShapeDtypeStruct((count, FW, z * x), F32),
        ),
        in_specs=[WHOLE] * 4,
        out_specs=(WHOLE, WHOLE),
        scratch_shapes=[pltpu.VMEM((count, z + FW, x, y), F32), pltpu.VMEM((z, 2 * x, y), F32)],
        compiler_params=PARAMS,
        cost_estimate=pl.CostEstimate(flops=count * z * x * y * 100, bytes_accessed=40 * z * x * y * 4, transcendentals=0),
    )(before, own, after, partial)


def hat(size, row, offset):
    distance = lax.broadcasted_iota(jnp.int32, (size, row.shape[1]), 0) - row
    return jnp.where(distance == 0, 1.0 - offset, jnp.where(distance == 1, offset, 0.0))


def hat_kernel(sizes, asked, w_high, w_low, w_y):
    size_z, size_x, size_y = sizes
    blocks = asked.shape[2] // BLOCK

    def weights(n, carry):
        group = n // blocks
        here = pl.ds(pl.multiple_of((n % blocks) * BLOCK, BLOCK), BLOCK)
        there = pl.ds(pl.multiple_of(n * BLOCK, BLOCK), BLOCK)
        cell = asked[group, 0:1, here].astype(jnp.int32)
        wx, wy, wz = (asked[group, k : k + 1, here] for k in (1, 2, 3))
        in_z = hat(size_z, cell // (size_x * size_y), wz)
        in_x = hat(size_x, (cell // size_y) % size_x, wx)
        w_y[:, there] = hat(size_y, cell % size_y, wy)
        for z in range(size_z):
            high, low = split2(in_z[z : z + 1] * in_x)
            w_high[z * size_x : (z + 1) * size_x, there] = high
            w_low[z * size_x : (z + 1) * size_x, there] = low
        return carry

    lax.fori_loop(0, asked.shape[0] * blocks, weights, 0)


def hats(asked, sizes):
    size_z, size_x, size_y = sizes
    count = asked.shape[0] * asked.shape[2]

    def kernel(*refs):
        hat_kernel(sizes, *refs)

    return pl.pallas_call(
        kernel,
        out_shape=(
            jax.ShapeDtypeStruct((size_z * size_x, count), BF16),
            jax.ShapeDtypeStruct((size_z * size_x, count), BF16),
            jax.ShapeDtypeStruct((size_y, count), F32),
        ),
        in_specs=[WHOLE],
        out_specs=(WHOLE,) * 3,
        compiler_params=PARAMS,
        cost_estimate=pl.CostEstimate(flops=count * 2000, bytes_accessed=count * 1600, transcendentals=0),
    )(asked)


def y_kernel(band, *refs):
    *parts, out = refs
    start = 0
    for fields in parts:

        def filtered(f, carry, fields=fields, start=start):
            out[start + f] = lax.dot_general(
                band[...], fields[f], (((1,), (1,)), ((), ())),
                precision=lax.Precision.HIGHEST, preferred_element_type=F32,
            )
            return carry

        lax.fori_loop(0, fields.shape[0], filtered, 0)
        start = start + fields.shape[0]


def along_y(band, parts):
    _, cells, size_y = parts[0].shape
    return pl.pallas_call(
        y_kernel,
        out_shape=jax.ShapeDtypeStruct((9, size_y, cells), F32),
        in_specs=[WHOLE] * (1 + len(parts)),
        out_specs=WHOLE,
        compiler_params=PARAMS,
        cost_estimate=pl.CostEstimate(flops=9 * 12 * size_y * size_y * cells, bytes_accessed=18 * cells * size_y * 4, transcendentals=0),
    )(band, *parts)


def sample_kernel(partial, first, second, band, w_high, w_low, w_y, out, field_high, field_low):
    size_y = partial.shape[1]
    blocks = out.shape[2] // BLOCK

    def smooth(f):
        strips = first[f] if f < first.shape[0] else second[f - first.shape[0]]
        return partial[f] + jnp.dot(
            band[...], strips, precision=lax.Precision.HIGHEST, preferred_element_type=F32
        )

    mean = [smooth(k) for k in range(3)]
    for k, (a, b) in enumerate(PAIRS):
        high, low = split2(smooth(3 + k) - mean[a] * mean[b])
        field_high[k * size_y : (k + 1) * size_y] = high
        field_low[k * size_y : (k + 1) * size_y] = low

    def sample(n, carry):
        group = n // blocks
        here = pl.ds(pl.multiple_of((n % blocks) * BLOCK, BLOCK), BLOCK)
        there = pl.ds(pl.multiple_of(n * BLOCK, BLOCK), BLOCK)
        high = w_high[:, there]
        wide = jnp.dot(field_high[...], high, preferred_element_type=F32)
        wide = wide + jnp.dot(field_low[...], high, preferred_element_type=F32)
        wide = wide + jnp.dot(field_high[...], w_low[:, there], preferred_element_type=F32)
        in_y = w_y[:, there]
        for k in range(6):
            part = wide[k * size_y : (k + 1) * size_y] * in_y
            out[group, k : k + 1, here] = jnp.sum(part, axis=0, keepdims=True)
        out[group, 6:ROWS, here] = jnp.zeros((ROWS - 6, BLOCK), F32)
        return carry

    lax.fori_loop(0, out.shape[0] * blocks, sample, 0, unroll=4)


def samples(partial, first, second, band, w_high, w_low, w_y, groups):
    _, size_y, cells = partial.shape
    count = w_y.shape[1]
    return pl.pallas_call(
        sample_kernel,
        out_shape=jax.ShapeDtypeStruct((groups, ROWS, count // groups), F32),
        in_specs=[WHOLE] * 7,
        out_specs=WHOLE,
        scratch_shapes=[pltpu.VMEM((6 * size_y, cells), BF16), pltpu.VMEM((6 * size_y, cells), BF16)],
        compiler_params=PARAMS,
        cost_estimate=pl.CostEstimate(flops=6 * size_y * cells * count * 6, bytes_accessed=8 * 1024 * 1024, transcendentals=0),
    )(partial, first, second, band, w_high, w_low, w_y)


def route_kernel(owners, capacity, record, out, slot_out, target_out):
    count = record.shape[1]
    target = record[0:1].astype(jnp.int32)
    named = lax.broadcasted_iota(jnp.int32, (owners, count), 0) == target
    earlier = lax.broadcasted_iota(jnp.int32, (count, count), 0) < lax.broadcasted_iota(jnp.int32, (count, count), 1)
    before = jnp.dot(
        jnp.where(named, 1.0, 0.0).astype(BF16), jnp.where(earlier, 1.0, 0.0).astype(BF16),
        preferred_element_type=F32,
    )
    rank = jnp.sum(jnp.where(named, before, 0.0), axis=0, keepdims=True).astype(jnp.int32)
    target_out[...] = target
    slot = lax.broadcasted_iota(jnp.int32, (capacity, count), 0) == rank
    slot = jnp.where(slot, 1.0, 0.0).astype(BF16)
    slot_out[...] = slot
    total = jnp.zeros((owners * 8, capacity), F32)
    for part in split3(record[...]):
        part = part.astype(F32)
        spread = jnp.concatenate(
            [jnp.where(target == o, part, 0.0) for o in range(owners)], axis=0
        ).astype(BF16)
        total = total + lax.dot_general(spread, slot, (((1,), (1,)), ((), ())), preferred_element_type=F32)
    for o in range(owners):
        out[o] = total[o * 8 + 1 : o * 8 + 5]


def route(record, owners, capacity):
    count = record.shape[1]

    def kernel(*refs):
        route_kernel(owners, capacity, *refs)

    return pl.pallas_call(
        kernel,
        out_shape=(
            jax.ShapeDtypeStruct((owners, 4, capacity), F32),
            jax.ShapeDtypeStruct((capacity, count), BF16),
            jax.ShapeDtypeStruct((1, count), jnp.int32),
        ),
        in_specs=[WHOLE],
        out_specs=(WHOLE,) * 3,
        compiler_params=PARAMS,
        cost_estimate=pl.CostEstimate(flops=10 * count * count * owners, bytes_accessed=count * 4 * 40, transcendentals=0),
    )(record)


def return_kernel(owners, back, slot, owner, out):
    count = owner.shape[1]
    picked = jnp.zeros((owners * ROWS, count), F32)
    for part in split3(back[...]):
        picked = picked + jnp.dot(part, slot[...], preferred_element_type=F32)
    target = owner[...]
    total = jnp.zeros((ROWS, count), F32)
    for o in range(owners):
        total = total + jnp.where(target == o, picked[o * ROWS : (o + 1) * ROWS], 0.0)
    out[...] = total[:6]


def returned(back, slot, owner, owners):
    count = owner.shape[1]

    def kernel(*refs):
        return_kernel(owners, *refs)

    return pl.pallas_call(
        kernel,
        out_shape=jax.ShapeDtypeStruct((6, count), F32),
        in_specs=[WHOLE] * 3,
        out_specs=WHOLE,
        compiler_params=PARAMS,
        cost_estimate=pl.CostEstimate(flops=6 * owners * ROWS * back.shape[1] * count, bytes_accessed=count * 100, transcendentals=0),
    )(back, slot, owner)


def y_band(size_y):
    radius = FW // 2
    place = np.concatenate([np.arange(size_y + radius), np.arange(-radius, 0)])
    offset = place[None, :] - np.arange(size_y)[:, None] + radius
    g = np.array(taps())
    band = np.where((offset >= 0) & (offset <= FW), g[np.clip(offset, 0, FW)], 0.0)
    return band[:, :size_y].astype(np.float32), band[:, size_y:].astype(np.float32)


def y_strips(edges):
    radius = FW // 2
    devices = lax.axis_size("gy")
    if devices == 2:
        return lax.ppermute(edges, "gy", [(0, 1), (1, 0)])
    following = shifted(edges[:, :radius], "gy", -1)
    previous = shifted(edges[:, radius:], "gy", 1)
    return jnp.concatenate([following, previous], axis=1)


def on_device(velocity, owner, cell_x, cell_y, cell_z, query_weights):
    _, size_z, size_x, size_y = velocity.shape
    owners = lax.axis_size("gx") * lax.axis_size("gy")
    count = owner.shape[0]
    capacity = 4 * count // owners

    sizes = (size_z, size_x, size_y)
    folded = capacity % BLOCK != 0

    sizes = (size_z, size_x, size_y)
    folded = capacity % BLOCK != 0

    row = lax.broadcasted_iota(jnp.int32, (8, count), 0)
    cell = (cell_z * size_x + cell_x) * size_y + cell_y
    record = jnp.pad(query_weights, ((2, 3), (0, 0)))
    record = jnp.where(row == 1, cell[None].astype(F32), record)
    record = jnp.where(row == 0, owner.reshape(1, count).astype(F32), record)
    sent, slot, target = route(record, owners, capacity)

    right = shifted(velocity, "gx", -1)
    left = shifted(after(velocity, record), "gx", 1)
    own_halo = neighbours(velocity, "gz")
    right = relayed(after(right, own_halo, sent))
    asked = lax.all_to_all(sent, ("gx", "gy"), split_axis=0, concat_axis=0, tiled=True)
    own_z = along_z(own_halo[0], velocity, own_halo[1])
    left = relayed(after(left, own_z, asked))
    partial = along_x_first(own_z, along_z(*right))
    if folded:
        asked = asked.transpose(1, 0, 2).reshape(1, 4, owners * capacity)
    weights = hats(asked, sizes)
    partial = after(partial, weights)
    band_own, band_strips = y_band(size_y)
    first, edges = along_x_last(tuple(range(5)), *left, partial)
    first_strips = y_strips(edges)
    second, edges = along_x_last(tuple(range(5, 9)), *left, partial)
    second_strips = y_strips(edges)
    partial = along_y(jnp.asarray(band_own), (first, second))
    values = samples(partial, first_strips, second_strips, jnp.asarray(band_strips), *weights, asked.shape[0])
    if folded:
        values = values.reshape(ROWS, owners, capacity).transpose(1, 0, 2)
    back = lax.all_to_all(values, ("gx", "gy"), split_axis=0, concat_axis=0, tiled=True)
    return returned(back.reshape(owners * ROWS, capacity), slot, target, owners)


def solution(mesh):
    placed = (
        P(None, "gz", "gx", "gy"),
        P(("gx", "gy", "gz"), None),
        P(("gx", "gy", "gz")),
        P(("gx", "gy", "gz")),
        P(("gx", "gy", "gz")),
        P(None, ("gx", "gy", "gz")),
    )
    return jax.shard_map(
        on_device,
        mesh=mesh,
        in_specs=placed,
        out_specs=P(None, ("gx", "gy", "gz")),
        check_vma=False,
    )
```

```python
import math

import jax
import jax.numpy as jnp
import numpy as np
from jax import lax
from jax.experimental import pallas as pl
from jax.experimental.pallas import tpu as pltpu
from jax.sharding import PartitionSpec as P

FW = 32
PAIRS = ((0, 0), (0, 1), (0, 2), (1, 1), (1, 2), (2, 2))
ROWS = 8
BLOCK = 256
F32 = jnp.float32
BF16 = jnp.bfloat16
WHOLE = pl.BlockSpec(memory_space=pltpu.VMEM)
PARAMS = pltpu.CompilerParams(vmem_limit_bytes=24 * 1024 * 1024)


def taps():
    radius = FW // 2
    values = [math.exp(-6.0 * (m - radius) ** 2 / FW**2) for m in range(2 * radius + 1)]
    return [v / sum(values) for v in values]


def shifted(x, axis, step):
    devices = lax.axis_size(axis)
    return lax.ppermute(x, axis, [(i, (i + step) % devices) for i in range(devices)])


def neighbours(x, axis):
    return shifted(x, axis, 1), shifted(x, axis, -1)


def after(x, *others):
    return lax.optimization_barrier((x, others))[0]


def relayed(brick):
    previous, following = neighbours(brick, "gz")
    return previous, brick, following


def symmetric(values, centre):
    radius = FW // 2
    g = taps()
    totals = [g[radius] * values[centre]]
    for m in range(1, radius + 1):
        term = g[radius + m] * (values[centre - m] + values[centre + m])
        if m < 4:
            totals.append(term)
        else:
            totals[m % 4] = totals[m % 4] + term
    return (totals[0] + totals[1]) + (totals[2] + totals[3])


def split2(x):
    high = x.astype(BF16)
    return high, (x - high.astype(F32)).astype(BF16)


def split3(x):
    high, rest = x.astype(BF16), None
    rest = x - high.astype(F32)
    middle = rest.astype(BF16)
    return high, middle, (rest - middle.astype(F32)).astype(BF16)


def form_products(before, own, after, wide, fields=tuple(range(9))):
    layers = own.shape[1]
    radius = FW // 2
    for part, (ref, skip) in enumerate(((before, layers - radius), (own, 0), (after, 0))):
        place = (0, radius, radius + layers)[part]

        def products(z, carry, ref=ref, skip=skip, place=place):
            u = [ref[k, z + skip] for k in range(3)]
            u = u + [u[a] * u[b] for a, b in PAIRS]
            for n, f in enumerate(fields):
                wide[n, z + place] = u[f]
            return carry

        lax.fori_loop(0, layers if part == 1 else radius, products, 0, unroll=4)


def z_kernel(before, own, after, out, wide):
    layers, size_x = own.shape[1], own.shape[2]
    radius = FW // 2
    form_products(before, own, after, wide)

    def filtered(f, carry):
        for x in range(0, size_x, 8):
            values = [wide[f, z, x : x + 8] for z in range(layers + 2 * radius)]
            for z in range(layers):
                out[f, z, x : x + 8] = symmetric(values, z + radius)
        return carry

    lax.fori_loop(0, 9, filtered, 0)


def along_z(before, own, after):
    _, z, x, y = own.shape
    return pl.pallas_call(
        z_kernel,
        out_shape=jax.ShapeDtypeStruct((9, z, x, y), F32),
        in_specs=[WHOLE] * 3,
        out_specs=WHOLE,
        scratch_shapes=[pltpu.VMEM((9, z + FW, x, y), F32)],
        compiler_params=PARAMS,
        cost_estimate=pl.CostEstimate(flops=9 * z * x * y * 66, bytes_accessed=21 * z * x * y * 4, transcendentals=0),
    )(before, own, after)


def first_kernel(own, right, out, wide):
    layers, size_x = own.shape[1:3]
    radius = FW // 2
    empty = jnp.zeros((radius, own.shape[3]), F32)
    for z in range(layers):
        wide[z, :radius] = empty

    def filtered(f, carry):
        for z in range(layers):
            wide[z, radius : radius + size_x] = own[f, z]
            wide[z, radius + size_x :] = right[f, z, :radius]
        for z in range(layers):
            values = [wide[z, i : i + 8] for i in range(size_x + FW - 7)]
            for x in range(0, size_x, 8):
                out[f, z * size_x + x : z * size_x + x + 8] = symmetric(values, x + radius)
        return carry

    lax.fori_loop(0, 9, filtered, 0)


def along_x_first(own, right):
    _, z, x, y = own.shape
    return pl.pallas_call(
        first_kernel,
        out_shape=jax.ShapeDtypeStruct((9, z * x, y), F32),
        in_specs=[WHOLE] * 2,
        out_specs=WHOLE,
        scratch_shapes=[pltpu.VMEM((z, x + FW, y), F32)],
        compiler_params=PARAMS,
        cost_estimate=pl.CostEstimate(flops=9 * z * x * y * 66, bytes_accessed=30 * z * x * y * 4, transcendentals=0),
    )(own, right)


def last_kernel(fields, before, own, after, partial, out, strips, wide, padded):
    layers, size_x, size_y = own.shape[1:]
    radius = FW // 2
    g = taps()
    form_products(before, own, after, wide, fields)
    empty = jnp.zeros((size_x, size_y), F32)
    for z in range(layers):
        padded[z, size_x:] = empty

    def filtered(f, carry):
        for x in range(0, size_x, 8):
            values = [wide[f, z, x : x + 8] for z in range(layers + 2 * radius)]
            for z in range(layers):
                padded[z, x : x + 8] = symmetric(values, z + radius)
        for z in range(layers):
            for x in range(0, size_x, 8):
                added = [
                    g[radius - size_x + k] * padded[z, x + k : x + k + 8]
                    for k in range(size_x - radius, size_x - x)
                ]
                while len(added) > 1:
                    added = [p + q for p, q in zip(added[::2], added[1::2])] + added[len(added) // 2 * 2 :]
                row = z * size_x + x
                out[f, row : row + 8] = partial[fields[0] + f, row : row + 8] + added[0]
        for n in range(0, layers * size_x, 128):
            turned = out[f, n : n + 128].T
            strips[f, :radius, n : n + 128] = turned[:radius]
            strips[f, radius:, n : n + 128] = turned[size_y - radius :]
        return carry

    lax.fori_loop(0, len(fields), filtered, 0)


def along_x_last(fields, before, own, after, partial):
    _, z, x, y = own.shape
    count = len(fields)

    def kernel(*refs):
        last_kernel(fields, *refs)

    return pl.pallas_call(
        kernel,
        out_shape=(
            jax.ShapeDtypeStruct((count, z * x, y), F32),
            jax.ShapeDtypeStruct((count, FW, z * x), F32),
        ),
        in_specs=[WHOLE] * 4,
        out_specs=(WHOLE, WHOLE),
        scratch_shapes=[pltpu.VMEM((count, z + FW, x, y), F32), pltpu.VMEM((z, 2 * x, y), F32)],
        compiler_params=PARAMS,
        cost_estimate=pl.CostEstimate(flops=count * z * x * y * 100, bytes_accessed=40 * z * x * y * 4, transcendentals=0),
    )(before, own, after, partial)


def hat(size, row, offset):
    distance = lax.broadcasted_iota(jnp.int32, (size, row.shape[1]), 0) - row
    return jnp.where(distance == 0, 1.0 - offset, jnp.where(distance == 1, offset, 0.0))


def hat_kernel(sizes, asked, w_high, w_low, w_y):
    size_z, size_x, size_y = sizes
    blocks = asked.shape[2] // BLOCK

    def weights(n, carry):
        group = n // blocks
        here = pl.ds(pl.multiple_of((n % blocks) * BLOCK, BLOCK), BLOCK)
        there = pl.ds(pl.multiple_of(n * BLOCK, BLOCK), BLOCK)
        cell = asked[group, 0:1, here].astype(jnp.int32)
        wx, wy, wz = (asked[group, k : k + 1, here] for k in (1, 2, 3))
        in_z = hat(size_z, cell // (size_x * size_y), wz)
        in_x = hat(size_x, (cell // size_y) % size_x, wx)
        w_y[:, there] = hat(size_y, cell % size_y, wy)
        for z in range(size_z):
            high, low = split2(in_z[z : z + 1] * in_x)
            w_high[z * size_x : (z + 1) * size_x, there] = high
            w_low[z * size_x : (z + 1) * size_x, there] = low
        return carry

    lax.fori_loop(0, asked.shape[0] * blocks, weights, 0)


def hats(asked, sizes):
    size_z, size_x, size_y = sizes
    count = asked.shape[0] * asked.shape[2]

    def kernel(*refs):
        hat_kernel(sizes, *refs)

    return pl.pallas_call(
        kernel,
        out_shape=(
            jax.ShapeDtypeStruct((size_z * size_x, count), BF16),
            jax.ShapeDtypeStruct((size_z * size_x, count), BF16),
            jax.ShapeDtypeStruct((size_y, count), F32),
        ),
        in_specs=[WHOLE],
        out_specs=(WHOLE,) * 3,
        compiler_params=PARAMS,
        cost_estimate=pl.CostEstimate(flops=count * 2000, bytes_accessed=count * 1600, transcendentals=0),
    )(asked)


def y_kernel(band, *refs):
    *parts, out = refs
    start = 0
    for fields in parts:

        def filtered(f, carry, fields=fields, start=start):
            out[start + f] = lax.dot_general(
                band[...], fields[f], (((1,), (1,)), ((), ())),
                precision=lax.Precision.HIGHEST, preferred_element_type=F32,
            )
            return carry

        lax.fori_loop(0, fields.shape[0], filtered, 0)
        start = start + fields.shape[0]


def along_y(band, parts):
    _, cells, size_y = parts[0].shape
    return pl.pallas_call(
        y_kernel,
        out_shape=jax.ShapeDtypeStruct((9, size_y, cells), F32),
        in_specs=[WHOLE] * (1 + len(parts)),
        out_specs=WHOLE,
        compiler_params=PARAMS,
        cost_estimate=pl.CostEstimate(flops=9 * 12 * size_y * size_y * cells, bytes_accessed=18 * cells * size_y * 4, transcendentals=0),
    )(band, *parts)


def sample_kernel(partial, first, second, band, w_high, w_low, w_y, out, field_high, field_low):
    size_y = partial.shape[1]
    blocks = out.shape[2] // BLOCK

    def smooth(f):
        strips = first[f] if f < first.shape[0] else second[f - first.shape[0]]
        return partial[f] + jnp.dot(
            band[...], strips, precision=lax.Precision.HIGHEST, preferred_element_type=F32
        )

    mean = [smooth(k) for k in range(3)]
    for k, (a, b) in enumerate(PAIRS):
        high, low = split2(smooth(3 + k) - mean[a] * mean[b])
        field_high[k * size_y : (k + 1) * size_y] = high
        field_low[k * size_y : (k + 1) * size_y] = low

    def sample(n, carry):
        group = n // blocks
        here = pl.ds(pl.multiple_of((n % blocks) * BLOCK, BLOCK), BLOCK)
        there = pl.ds(pl.multiple_of(n * BLOCK, BLOCK), BLOCK)
        high = w_high[:, there]
        wide = jnp.dot(field_high[...], high, preferred_element_type=F32)
        wide = wide + jnp.dot(field_low[...], high, preferred_element_type=F32)
        wide = wide + jnp.dot(field_high[...], w_low[:, there], preferred_element_type=F32)
        in_y = w_y[:, there]
        for k in range(6):
            part = wide[k * size_y : (k + 1) * size_y] * in_y
            out[group, k : k + 1, here] = jnp.sum(part, axis=0, keepdims=True)
        out[group, 6:ROWS, here] = jnp.zeros((ROWS - 6, BLOCK), F32)
        return carry

    lax.fori_loop(0, out.shape[0] * blocks, sample, 0, unroll=16)


def samples(partial, first, second, band, w_high, w_low, w_y, groups):
    _, size_y, cells = partial.shape
    count = w_y.shape[1]
    return pl.pallas_call(
        sample_kernel,
        out_shape=jax.ShapeDtypeStruct((groups, ROWS, count // groups), F32),
        in_specs=[WHOLE] * 7,
        out_specs=WHOLE,
        scratch_shapes=[pltpu.VMEM((6 * size_y, cells), BF16), pltpu.VMEM((6 * size_y, cells), BF16)],
        compiler_params=PARAMS,
        cost_estimate=pl.CostEstimate(flops=6 * size_y * cells * count * 6, bytes_accessed=8 * 1024 * 1024, transcendentals=0),
    )(partial, first, second, band, w_high, w_low, w_y)


def route_kernel(owners, capacity, record, out, slot_out, target_out):
    count = record.shape[1]
    target = record[0:1].astype(jnp.int32)
    named = lax.broadcasted_iota(jnp.int32, (owners, count), 0) == target
    earlier = lax.broadcasted_iota(jnp.int32, (count, count), 0) < lax.broadcasted_iota(jnp.int32, (count, count), 1)
    before = jnp.dot(
        jnp.where(named, 1.0, 0.0).astype(BF16), jnp.where(earlier, 1.0, 0.0).astype(BF16),
        preferred_element_type=F32,
    )
    rank = jnp.sum(jnp.where(named, before, 0.0), axis=0, keepdims=True).astype(jnp.int32)
    target_out[...] = target
    slot = lax.broadcasted_iota(jnp.int32, (capacity, count), 0) == rank
    slot = jnp.where(slot, 1.0, 0.0).astype(BF16)
    slot_out[...] = slot
    total = jnp.zeros((owners * 8, capacity), F32)
    for part in split3(record[...]):
        part = part.astype(F32)
        spread = jnp.concatenate(
            [jnp.where(target == o, part, 0.0) for o in range(owners)], axis=0
        ).astype(BF16)
        total = total + lax.dot_general(spread, slot, (((1,), (1,)), ((), ())), preferred_element_type=F32)
    for o in range(owners):
        out[o] = total[o * 8 + 1 : o * 8 + 5]


def route(record, owners, capacity):
    count = record.shape[1]

    def kernel(*refs):
        route_kernel(owners, capacity, *refs)

    return pl.pallas_call(
        kernel,
        out_shape=(
            jax.ShapeDtypeStruct((owners, 4, capacity), F32),
            jax.ShapeDtypeStruct((capacity, count), BF16),
            jax.ShapeDtypeStruct((1, count), jnp.int32),
        ),
        in_specs=[WHOLE],
        out_specs=(WHOLE,) * 3,
        compiler_params=PARAMS,
        cost_estimate=pl.CostEstimate(flops=10 * count * count * owners, bytes_accessed=count * 4 * 40, transcendentals=0),
    )(record)


def return_kernel(owners, back, slot, owner, out):
    count = owner.shape[1]
    picked = jnp.zeros((owners * ROWS, count), F32)
    for part in split2(back[...]):
        picked = picked + jnp.dot(part, slot[...], preferred_element_type=F32)
    target = owner[...]
    total = jnp.zeros((ROWS, count), F32)
    for o in range(owners):
        total = total + jnp.where(target == o, picked[o * ROWS : (o + 1) * ROWS], 0.0)
    out[...] = total[:6]


def returned(back, slot, owner, owners):
    count = owner.shape[1]

    def kernel(*refs):
        return_kernel(owners, *refs)

    return pl.pallas_call(
        kernel,
        out_shape=jax.ShapeDtypeStruct((6, count), F32),
        in_specs=[WHOLE] * 3,
        out_specs=WHOLE,
        compiler_params=PARAMS,
        cost_estimate=pl.CostEstimate(flops=6 * owners * ROWS * back.shape[1] * count, bytes_accessed=count * 100, transcendentals=0),
    )(back, slot, owner)


def y_band(size_y):
    radius = FW // 2
    place = np.concatenate([np.arange(size_y + radius), np.arange(-radius, 0)])
    offset = place[None, :] - np.arange(size_y)[:, None] + radius
    g = np.array(taps())
    band = np.where((offset >= 0) & (offset <= FW), g[np.clip(offset, 0, FW)], 0.0)
    return band[:, :size_y].astype(np.float32), band[:, size_y:].astype(np.float32)


def y_strips(edges):
    radius = FW // 2
    devices = lax.axis_size("gy")
    if devices == 2:
        return lax.ppermute(edges, "gy", [(0, 1), (1, 0)])
    following = shifted(edges[:, :radius], "gy", -1)
    previous = shifted(edges[:, radius:], "gy", 1)
    return jnp.concatenate([following, previous], axis=1)


def on_device(velocity, owner, cell_x, cell_y, cell_z, query_weights):
    _, size_z, size_x, size_y = velocity.shape
    owners = lax.axis_size("gx") * lax.axis_size("gy")
    count = owner.shape[0]
    capacity = 4 * count // owners

    sizes = (size_z, size_x, size_y)
    folded = capacity % BLOCK != 0

    sizes = (size_z, size_x, size_y)
    folded = capacity % BLOCK != 0

    row = lax.broadcasted_iota(jnp.int32, (8, count), 0)
    flat = (jnp.broadcast_to(k.reshape(1, count), (8, count)) for k in (owner, cell_x, cell_y, cell_z))
    named, in_x, in_y, in_z = flat
    cell = (in_z * size_x + in_x) * size_y + in_y
    record = jnp.pad(query_weights, ((2, 3), (0, 0)))
    record = jnp.where(row > 1, record, jnp.where(row == 1, cell, named).astype(F32))
    sent, slot, target = route(record, owners, capacity)

    right = shifted(velocity, "gx", -1)
    left = shifted(after(velocity, record), "gx", 1)
    own_halo = shifted(velocity, "gz", 1), shifted(after(velocity, record), "gz", -1)
    right = relayed(right)
    asked = lax.all_to_all(sent, ("gx", "gy"), split_axis=0, concat_axis=0, tiled=True)
    own_z = along_z(own_halo[0], velocity, own_halo[1])
    left = (shifted(after(left, own_z, asked), "gz", 1), left, shifted(own_halo[1], "gx", 1))
    partial = along_x_first(own_z, along_z(*right))
    if folded:
        asked = asked.transpose(1, 0, 2).reshape(1, 4, owners * capacity)
    weights = hats(asked, sizes)
    partial = after(partial, weights)
    band_own, band_strips = y_band(size_y)
    first, edges = along_x_last(tuple(range(5)), *left, partial)
    first_strips = y_strips(edges)
    second, edges = along_x_last(tuple(range(5, 9)), *left, partial)
    second_strips = y_strips(edges)
    partial = along_y(jnp.asarray(band_own), (first, second))
    values = samples(partial, first_strips, second_strips, jnp.asarray(band_strips), *weights, asked.shape[0])
    if folded:
        values = values.reshape(ROWS, owners, capacity).transpose(1, 0, 2)
    back = lax.all_to_all(values, ("gx", "gy"), split_axis=0, concat_axis=0, tiled=True)
    return returned(back.reshape(owners * ROWS, capacity), slot, target, owners)


def solution(mesh):
    placed = (
        P(None, "gz", "gx", "gy"),
        P(("gx", "gy", "gz"), None),
        P(("gx", "gy", "gz")),
        P(("gx", "gy", "gz")),
        P(("gx", "gy", "gz")),
        P(None, ("gx", "gy", "gz")),
    )
    return jax.shard_map(
        on_device,
        mesh=mesh,
        in_specs=placed,
        out_specs=P(None, ("gx", "gy", "gz")),
        check_vma=False,
    )
```

```python
import math

import jax
import jax.numpy as jnp
import numpy as np
from jax import lax
from jax.experimental import pallas as pl
from jax.experimental.pallas import tpu as pltpu
from jax.sharding import PartitionSpec as P

FW = 32
PAIRS = ((0, 0), (0, 1), (0, 2), (1, 1), (1, 2), (2, 2))
ROWS = 8
BLOCK = 256
F32 = jnp.float32
BF16 = jnp.bfloat16
WHOLE = pl.BlockSpec(memory_space=pltpu.VMEM)
PARAMS = pltpu.CompilerParams(vmem_limit_bytes=24 * 1024 * 1024)


def taps():
    radius = FW // 2
    values = [math.exp(-6.0 * (m - radius) ** 2 / FW**2) for m in range(2 * radius + 1)]
    return [v / sum(values) for v in values]


def shifted(x, axis, step):
    devices = lax.axis_size(axis)
    return lax.ppermute(x, axis, [(i, (i + step) % devices) for i in range(devices)])


def neighbours(x, axis):
    return shifted(x, axis, 1), shifted(x, axis, -1)


def after(x, *others):
    return lax.optimization_barrier((x, others))[0]


def relayed(brick):
    previous, following = neighbours(brick, "gz")
    return previous, brick, following


def symmetric(values, centre):
    radius = FW // 2
    g = taps()
    totals = [g[radius] * values[centre]]
    for m in range(1, radius + 1):
        term = g[radius + m] * (values[centre - m] + values[centre + m])
        if m < 4:
            totals.append(term)
        else:
            totals[m % 4] = totals[m % 4] + term
    return (totals[0] + totals[1]) + (totals[2] + totals[3])


def split2(x):
    high = x.astype(BF16)
    return high, (x - high.astype(F32)).astype(BF16)


def split3(x):
    high, rest = x.astype(BF16), None
    rest = x - high.astype(F32)
    middle = rest.astype(BF16)
    return high, middle, (rest - middle.astype(F32)).astype(BF16)


def form_products(before, own, after, wide, fields=tuple(range(9))):
    layers = own.shape[1]
    radius = FW // 2
    for part, (ref, skip) in enumerate(((before, layers - radius), (own, 0), (after, 0))):
        place = (0, radius, radius + layers)[part]

        def products(z, carry, ref=ref, skip=skip, place=place):
            u = [ref[k, z + skip] for k in range(3)]
            u = u + [u[a] * u[b] for a, b in PAIRS]
            for n, f in enumerate(fields):
                wide[n, z + place] = u[f]
            return carry

        lax.fori_loop(0, layers if part == 1 else radius, products, 0, unroll=4)


def z_kernel(before, own, after, out, wide):
    layers, size_x = own.shape[1], own.shape[2]
    radius = FW // 2
    form_products(before, own, after, wide)

    def filtered(f, carry):
        for x in range(0, size_x, 8):
            values = [wide[f, z, x : x + 8] for z in range(layers + 2 * radius)]
            for z in range(layers):
                out[f, z, x : x + 8] = symmetric(values, z + radius)
        return carry

    lax.fori_loop(0, 9, filtered, 0)


def along_z(before, own, after):
    _, z, x, y = own.shape
    return pl.pallas_call(
        z_kernel,
        out_shape=jax.ShapeDtypeStruct((9, z, x, y), F32),
        in_specs=[WHOLE] * 3,
        out_specs=WHOLE,
        scratch_shapes=[pltpu.VMEM((9, z + FW, x, y), F32)],
        compiler_params=PARAMS,
        cost_estimate=pl.CostEstimate(flops=9 * z * x * y * 66, bytes_accessed=21 * z * x * y * 4, transcendentals=0),
    )(before, own, after)


def first_kernel(own, right, out, wide):
    layers, size_x = own.shape[1:3]
    radius = FW // 2
    empty = jnp.zeros((radius, own.shape[3]), F32)
    for z in range(layers):
        wide[z, :radius] = empty

    def filtered(f, carry):
        for z in range(layers):
            wide[z, radius : radius + size_x] = own[f, z]
            wide[z, radius + size_x :] = right[f, z, :radius]
        for z in range(layers):
            values = [wide[z, i : i + 8] for i in range(size_x + FW - 7)]
            for x in range(0, size_x, 8):
                out[f, z * size_x + x : z * size_x + x + 8] = symmetric(values, x + radius)
        return carry

    lax.fori_loop(0, 9, filtered, 0)


def along_x_first(own, right):
    _, z, x, y = own.shape
    return pl.pallas_call(
        first_kernel,
        out_shape=jax.ShapeDtypeStruct((9, z * x, y), F32),
        in_specs=[WHOLE] * 2,
        out_specs=WHOLE,
        scratch_shapes=[pltpu.VMEM((z, x + FW, y), F32)],
        compiler_params=PARAMS,
        cost_estimate=pl.CostEstimate(flops=9 * z * x * y * 66, bytes_accessed=30 * z * x * y * 4, transcendentals=0),
    )(own, right)


def last_kernel(fields, before, own, after, partial, out, strips, wide, padded):
    layers, size_x, size_y = own.shape[1:]
    radius = FW // 2
    g = taps()
    form_products(before, own, after, wide, fields)
    empty = jnp.zeros((size_x, size_y), F32)
    for z in range(layers):
        padded[z, size_x:] = empty

    def filtered(f, carry):
        for x in range(0, size_x, 8):
            values = [wide[f, z, x : x + 8] for z in range(layers + 2 * radius)]
            for z in range(layers):
                padded[z, x : x + 8] = symmetric(values, z + radius)
        for z in range(layers):
            for x in range(0, size_x, 8):
                added = [
                    g[radius - size_x + k] * padded[z, x + k : x + k + 8]
                    for k in range(size_x - radius, size_x - x)
                ]
                while len(added) > 1:
                    added = [p + q for p, q in zip(added[::2], added[1::2])] + added[len(added) // 2 * 2 :]
                row = z * size_x + x
                out[f, row : row + 8] = partial[fields[0] + f, row : row + 8] + added[0]
        for n in range(0, layers * size_x, 128):
            turned = out[f, n : n + 128].T
            strips[f, :radius, n : n + 128] = turned[:radius]
            strips[f, radius:, n : n + 128] = turned[size_y - radius :]
        return carry

    lax.fori_loop(0, len(fields), filtered, 0)


def along_x_last(fields, before, own, after, partial):
    _, z, x, y = own.shape
    count = len(fields)

    def kernel(*refs):
        last_kernel(fields, *refs)

    return pl.pallas_call(
        kernel,
        out_shape=(
            jax.ShapeDtypeStruct((count, z * x, y), F32),
            jax.ShapeDtypeStruct((count, FW, z * x), F32),
        ),
        in_specs=[WHOLE] * 4,
        out_specs=(WHOLE, WHOLE),
        scratch_shapes=[pltpu.VMEM((count, z + FW, x, y), F32), pltpu.VMEM((z, 2 * x, y), F32)],
        compiler_params=PARAMS,
        cost_estimate=pl.CostEstimate(flops=count * z * x * y * 100, bytes_accessed=40 * z * x * y * 4, transcendentals=0),
    )(before, own, after, partial)


def hat(size, row, offset):
    distance = lax.broadcasted_iota(jnp.int32, (size, row.shape[1]), 0) - row
    return jnp.where(distance == 0, 1.0 - offset, jnp.where(distance == 1, offset, 0.0))


def hat_kernel(sizes, asked, w_high, w_low, w_y):
    size_z, size_x, size_y = sizes
    blocks = asked.shape[2] // BLOCK

    def weights(n, carry):
        group = n // blocks
        here = pl.ds(pl.multiple_of((n % blocks) * BLOCK, BLOCK), BLOCK)
        there = pl.ds(pl.multiple_of(n * BLOCK, BLOCK), BLOCK)
        cell = asked[group, 0:1, here].astype(jnp.int32)
        wx, wy, wz = (asked[group, k : k + 1, here] for k in (1, 2, 3))
        in_z = hat(size_z, cell // (size_x * size_y), wz)
        in_x = hat(size_x, (cell // size_y) % size_x, wx)
        w_y[:, there] = hat(size_y, cell % size_y, wy)
        for z in range(size_z):
            high, low = split2(in_z[z : z + 1] * in_x)
            w_high[z * size_x : (z + 1) * size_x, there] = high
            w_low[z * size_x : (z + 1) * size_x, there] = low
        return carry

    lax.fori_loop(0, asked.shape[0] * blocks, weights, 0)


def hats(asked, sizes):
    size_z, size_x, size_y = sizes
    count = asked.shape[0] * asked.shape[2]

    def kernel(*refs):
        hat_kernel(sizes, *refs)

    return pl.pallas_call(
        kernel,
        out_shape=(
            jax.ShapeDtypeStruct((size_z * size_x, count), BF16),
            jax.ShapeDtypeStruct((size_z * size_x, count), BF16),
            jax.ShapeDtypeStruct((size_y, count), F32),
        ),
        in_specs=[WHOLE],
        out_specs=(WHOLE,) * 3,
        compiler_params=PARAMS,
        cost_estimate=pl.CostEstimate(flops=count * 2000, bytes_accessed=count * 1600, transcendentals=0),
    )(asked)


def y_kernel(band, fields, *refs):
    out = refs[-1]

    def filtered(f, carry):
        total = lax.dot_general(
            band[...], fields[f], (((1,), (1,)), ((), ())),
            precision=lax.Precision.HIGHEST, preferred_element_type=F32,
        )
        if len(refs) > 1:
            total = total + jnp.dot(
                refs[0][...], refs[1][f], precision=lax.Precision.HIGHEST, preferred_element_type=F32
            )
        out[f] = total
        return carry

    lax.fori_loop(0, fields.shape[0], filtered, 0)


def along_y(band, fields, *edges):
    count, cells, size_y = fields.shape
    return pl.pallas_call(
        y_kernel,
        out_shape=jax.ShapeDtypeStruct((count, size_y, cells), F32),
        in_specs=[WHOLE] * (2 + len(edges)),
        out_specs=WHOLE,
        compiler_params=PARAMS,
        cost_estimate=pl.CostEstimate(flops=count * 12 * size_y * size_y * cells, bytes_accessed=2 * count * cells * size_y * 4, transcendentals=0),
    )(band, fields, *edges)


def sample_kernel(first, partial, strips, band, w_high, w_low, w_y, out, field_high, field_low):
    size_y = partial.shape[1]
    blocks = out.shape[2] // BLOCK

    def smooth(f):
        done = first.shape[0]
        if f < done:
            return first[f]
        return partial[f - done] + jnp.dot(
            band[...], strips[f - done], precision=lax.Precision.HIGHEST, preferred_element_type=F32
        )

    mean = [smooth(k) for k in range(3)]
    for k, (a, b) in enumerate(PAIRS):
        high, low = split2(smooth(3 + k) - mean[a] * mean[b])
        field_high[k * size_y : (k + 1) * size_y] = high
        field_low[k * size_y : (k + 1) * size_y] = low

    def sample(n, carry):
        group = n // blocks
        here = pl.ds(pl.multiple_of((n % blocks) * BLOCK, BLOCK), BLOCK)
        there = pl.ds(pl.multiple_of(n * BLOCK, BLOCK), BLOCK)
        high = w_high[:, there]
        wide = jnp.dot(field_high[...], high, preferred_element_type=F32)
        wide = wide + jnp.dot(field_low[...], high, preferred_element_type=F32)
        wide = wide + jnp.dot(field_high[...], w_low[:, there], preferred_element_type=F32)
        in_y = w_y[:, there]
        for k in range(6):
            part = wide[k * size_y : (k + 1) * size_y] * in_y
            out[group, k : k + 1, here] = jnp.sum(part, axis=0, keepdims=True)
        out[group, 6:ROWS, here] = jnp.zeros((ROWS - 6, BLOCK), F32)
        return carry

    lax.fori_loop(0, out.shape[0] * blocks, sample, 0, unroll=16)


def samples(first, partial, strips, band, w_high, w_low, w_y, groups):
    _, size_y, cells = partial.shape
    count = w_y.shape[1]
    return pl.pallas_call(
        sample_kernel,
        out_shape=jax.ShapeDtypeStruct((groups, ROWS, count // groups), F32),
        in_specs=[WHOLE] * 7,
        out_specs=WHOLE,
        scratch_shapes=[pltpu.VMEM((6 * size_y, cells), BF16), pltpu.VMEM((6 * size_y, cells), BF16)],
        compiler_params=PARAMS,
        cost_estimate=pl.CostEstimate(flops=6 * size_y * cells * count * 6, bytes_accessed=8 * 1024 * 1024, transcendentals=0),
    )(first, partial, strips, band, w_high, w_low, w_y)


def route_kernel(owners, capacity, record, out, slot_out, target_out):
    count = record.shape[1]
    target = record[0:1].astype(jnp.int32)
    named = lax.broadcasted_iota(jnp.int32, (owners, count), 0) == target
    earlier = lax.broadcasted_iota(jnp.int32, (count, count), 0) < lax.broadcasted_iota(jnp.int32, (count, count), 1)
    before = jnp.dot(
        jnp.where(named, 1.0, 0.0).astype(BF16), jnp.where(earlier, 1.0, 0.0).astype(BF16),
        preferred_element_type=F32,
    )
    rank = jnp.sum(jnp.where(named, before, 0.0), axis=0, keepdims=True).astype(jnp.int32)
    target_out[...] = target
    slot = lax.broadcasted_iota(jnp.int32, (capacity, count), 0) == rank
    slot = jnp.where(slot, 1.0, 0.0).astype(BF16)
    slot_out[...] = slot
    total = jnp.zeros((owners * 8, capacity), F32)
    for part in split3(record[...]):
        part = part.astype(F32)
        spread = jnp.concatenate(
            [jnp.where(target == o, part, 0.0) for o in range(owners)], axis=0
        ).astype(BF16)
        total = total + lax.dot_general(spread, slot, (((1,), (1,)), ((), ())), preferred_element_type=F32)
    for o in range(owners):
        out[o] = total[o * 8 + 1 : o * 8 + 5]


def route(record, owners, capacity):
    count = record.shape[1]

    def kernel(*refs):
        route_kernel(owners, capacity, *refs)

    return pl.pallas_call(
        kernel,
        out_shape=(
            jax.ShapeDtypeStruct((owners, 4, capacity), F32),
            jax.ShapeDtypeStruct((capacity, count), BF16),
            jax.ShapeDtypeStruct((1, count), jnp.int32),
        ),
        in_specs=[WHOLE],
        out_specs=(WHOLE,) * 3,
        compiler_params=PARAMS,
        cost_estimate=pl.CostEstimate(flops=10 * count * count * owners, bytes_accessed=count * 4 * 40, transcendentals=0),
    )(record)


def return_kernel(owners, back, slot, owner, out):
    count = owner.shape[1]
    picked = jnp.zeros((owners * ROWS, count), F32)
    for part in split2(back[...]):
        picked = picked + jnp.dot(part, slot[...], preferred_element_type=F32)
    target = owner[...]
    total = jnp.zeros((ROWS, count), F32)
    for o in range(owners):
        total = total + jnp.where(target == o, picked[o * ROWS : (o + 1) * ROWS], 0.0)
    out[...] = total[:6]


def returned(back, slot, owner, owners):
    count = owner.shape[1]

    def kernel(*refs):
        return_kernel(owners, *refs)

    return pl.pallas_call(
        kernel,
        out_shape=jax.ShapeDtypeStruct((6, count), F32),
        in_specs=[WHOLE] * 3,
        out_specs=WHOLE,
        compiler_params=PARAMS,
        cost_estimate=pl.CostEstimate(flops=6 * owners * ROWS * back.shape[1] * count, bytes_accessed=count * 100, transcendentals=0),
    )(back, slot, owner)


def y_band(size_y):
    radius = FW // 2
    place = np.concatenate([np.arange(size_y + radius), np.arange(-radius, 0)])
    offset = place[None, :] - np.arange(size_y)[:, None] + radius
    g = np.array(taps())
    band = np.where((offset >= 0) & (offset <= FW), g[np.clip(offset, 0, FW)], 0.0)
    return band[:, :size_y].astype(np.float32), band[:, size_y:].astype(np.float32)


def y_strips(edges):
    radius = FW // 2
    devices = lax.axis_size("gy")
    if devices == 2:
        return lax.ppermute(edges, "gy", [(0, 1), (1, 0)])
    following = shifted(edges[:, :radius], "gy", -1)
    previous = shifted(edges[:, radius:], "gy", 1)
    return jnp.concatenate([following, previous], axis=1)


def on_device(velocity, owner, cell_x, cell_y, cell_z, query_weights):
    _, size_z, size_x, size_y = velocity.shape
    owners = lax.axis_size("gx") * lax.axis_size("gy")
    count = owner.shape[0]
    capacity = 4 * count // owners

    sizes = (size_z, size_x, size_y)
    folded = capacity % BLOCK != 0

    sizes = (size_z, size_x, size_y)
    folded = capacity % BLOCK != 0

    row = lax.broadcasted_iota(jnp.int32, (8, count), 0)
    flat = (jnp.broadcast_to(k.reshape(1, count), (8, count)) for k in (owner, cell_x, cell_y, cell_z))
    named, in_x, in_y, in_z = flat
    cell = (in_z * size_x + in_x) * size_y + in_y
    record = jnp.pad(query_weights, ((2, 3), (0, 0)))
    record = jnp.where(row > 1, record, jnp.where(row == 1, cell, named).astype(F32))
    sent, slot, target = route(record, owners, capacity)

    right = shifted(velocity, "gx", -1)
    left = shifted(after(velocity, record), "gx", 1)
    own_halo = shifted(velocity, "gz", 1), shifted(after(velocity, record), "gz", -1)
    right = relayed(right)
    asked = lax.all_to_all(sent, ("gx", "gy"), split_axis=0, concat_axis=0, tiled=True)
    own_z = along_z(own_halo[0], velocity, own_halo[1])
    left = (shifted(after(left, own_z, asked), "gz", 1), left, shifted(own_halo[1], "gx", 1))
    partial = along_x_first(own_z, along_z(*right))
    if folded:
        asked = asked.transpose(1, 0, 2).reshape(1, 4, owners * capacity)
    weights = hats(asked, sizes)
    partial = after(partial, weights)
    band_own, band_strips = y_band(size_y)
    first, edges = along_x_last(tuple(range(5)), *left, partial)
    first_strips = y_strips(edges)
    second, edges = along_x_last(tuple(range(5, 9)), *left, partial)
    second_strips = y_strips(edges)
    band_own, band_strips = jnp.asarray(band_own), jnp.asarray(band_strips)
    partial = along_y(band_own, second)
    whole = along_y(band_own, after(first, partial), band_strips, first_strips)
    values = samples(whole, partial, second_strips, band_strips, *weights, asked.shape[0])
    if folded:
        values = values.reshape(ROWS, owners, capacity).transpose(1, 0, 2)
    back = lax.all_to_all(values, ("gx", "gy"), split_axis=0, concat_axis=0, tiled=True)
    return returned(back.reshape(owners * ROWS, capacity), slot, target, owners)


def solution(mesh):
    placed = (
        P(None, "gz", "gx", "gy"),
        P(("gx", "gy", "gz"), None),
        P(("gx", "gy", "gz")),
        P(("gx", "gy", "gz")),
        P(("gx", "gy", "gz")),
        P(None, ("gx", "gy", "gz")),
    )
    return jax.shard_map(
        on_device,
        mesh=mesh,
        in_specs=placed,
        out_specs=P(None, ("gx", "gy", "gz")),
        check_vma=False,
    )
```

```python
import math

import jax
import jax.numpy as jnp
import numpy as np
from jax import lax
from jax.experimental import pallas as pl
from jax.experimental.pallas import tpu as pltpu
from jax.sharding import PartitionSpec as P

FW = 32
PAIRS = ((0, 0), (0, 1), (0, 2), (1, 1), (1, 2), (2, 2))
ROWS = 8
BLOCK = 256
F32 = jnp.float32
BF16 = jnp.bfloat16
WHOLE = pl.BlockSpec(memory_space=pltpu.VMEM)
PARAMS = pltpu.CompilerParams(vmem_limit_bytes=24 * 1024 * 1024)


def taps():
    radius = FW // 2
    values = [math.exp(-6.0 * (m - radius) ** 2 / FW**2) for m in range(2 * radius + 1)]
    return [v / sum(values) for v in values]


def shifted(x, axis, step):
    devices = lax.axis_size(axis)
    return lax.ppermute(x, axis, [(i, (i + step) % devices) for i in range(devices)])


def neighbours(x, axis):
    return shifted(x, axis, 1), shifted(x, axis, -1)


def after(x, *others):
    return lax.optimization_barrier((x, others))[0]


def relayed(brick):
    previous, following = neighbours(brick, "gz")
    return previous, brick, following


def symmetric(values, centre):
    radius = FW // 2
    g = taps()
    totals = [g[radius] * values[centre]]
    for m in range(1, radius + 1):
        term = g[radius + m] * (values[centre - m] + values[centre + m])
        if m < 4:
            totals.append(term)
        else:
            totals[m % 4] = totals[m % 4] + term
    return (totals[0] + totals[1]) + (totals[2] + totals[3])


def split2(x):
    high = x.astype(BF16)
    return high, (x - high.astype(F32)).astype(BF16)


def split3(x):
    high, rest = x.astype(BF16), None
    rest = x - high.astype(F32)
    middle = rest.astype(BF16)
    return high, middle, (rest - middle.astype(F32)).astype(BF16)


def form_products(before, own, after, wide, fields=tuple(range(9))):
    layers = own.shape[1]
    radius = FW // 2
    for part, (ref, skip) in enumerate(((before, layers - radius), (own, 0), (after, 0))):
        place = (0, radius, radius + layers)[part]

        def products(z, carry, ref=ref, skip=skip, place=place):
            u = [ref[k, z + skip] for k in range(3)]
            u = u + [u[a] * u[b] for a, b in PAIRS]
            for n, f in enumerate(fields):
                wide[n, z + place] = u[f]
            return carry

        lax.fori_loop(0, layers if part == 1 else radius, products, 0, unroll=4)


def z_kernel(before, own, after, out, wide):
    layers, size_x = own.shape[1], own.shape[2]
    radius = FW // 2
    form_products(before, own, after, wide)

    def filtered(f, carry):
        for x in range(0, size_x, 8):
            values = [wide[f, z, x : x + 8] for z in range(layers + 2 * radius)]
            for z in range(layers):
                out[f, z, x : x + 8] = symmetric(values, z + radius)
        return carry

    lax.fori_loop(0, 9, filtered, 0)


def along_z(before, own, after):
    _, z, x, y = own.shape
    return pl.pallas_call(
        z_kernel,
        out_shape=jax.ShapeDtypeStruct((9, z, x, y), F32),
        in_specs=[WHOLE] * 3,
        out_specs=WHOLE,
        scratch_shapes=[pltpu.VMEM((9, z + FW, x, y), F32)],
        compiler_params=PARAMS,
        cost_estimate=pl.CostEstimate(flops=9 * z * x * y * 66, bytes_accessed=21 * z * x * y * 4, transcendentals=0),
    )(before, own, after)


def first_kernel(own, right, out, wide):
    layers, size_x = own.shape[1:3]
    radius = FW // 2
    empty = jnp.zeros((radius, own.shape[3]), F32)
    for z in range(layers):
        wide[z, :radius] = empty

    def filtered(f, carry):
        for z in range(layers):
            wide[z, radius : radius + size_x] = own[f, z]
            wide[z, radius + size_x :] = right[f, z, :radius]
        for z in range(layers):
            values = [wide[z, i : i + 8] for i in range(size_x + FW - 7)]
            for x in range(0, size_x, 8):
                out[f, z * size_x + x : z * size_x + x + 8] = symmetric(values, x + radius)
        return carry

    lax.fori_loop(0, 9, filtered, 0)


def along_x_first(own, right):
    _, z, x, y = own.shape
    return pl.pallas_call(
        first_kernel,
        out_shape=jax.ShapeDtypeStruct((9, z * x, y), F32),
        in_specs=[WHOLE] * 2,
        out_specs=WHOLE,
        scratch_shapes=[pltpu.VMEM((z, x + FW, y), F32)],
        compiler_params=PARAMS,
        cost_estimate=pl.CostEstimate(flops=9 * z * x * y * 66, bytes_accessed=30 * z * x * y * 4, transcendentals=0),
    )(own, right)


def last_kernel(fields, before, own, after, partial, out, strips, wide, padded):
    layers, size_x, size_y = own.shape[1:]
    radius = FW // 2
    g = taps()
    form_products(before, own, after, wide, fields)
    empty = jnp.zeros((size_x, size_y), F32)
    for z in range(layers):
        padded[z, size_x:] = empty

    def filtered(f, carry):
        for x in range(0, size_x, 8):
            values = [wide[f, z, x : x + 8] for z in range(layers + 2 * radius)]
            for z in range(layers):
                padded[z, x : x + 8] = symmetric(values, z + radius)
        for z in range(layers):
            for x in range(0, size_x, 8):
                added = [
                    g[radius - size_x + k] * padded[z, x + k : x + k + 8]
                    for k in range(size_x - radius, size_x - x)
                ]
                while len(added) > 1:
                    added = [p + q for p, q in zip(added[::2], added[1::2])] + added[len(added) // 2 * 2 :]
                row = z * size_x + x
                out[f, row : row + 8] = partial[fields[0] + f, row : row + 8] + added[0]
        for n in range(0, layers * size_x, 128):
            turned = out[f, n : n + 128].T
            strips[f, :radius, n : n + 128] = turned[:radius]
            strips[f, radius:, n : n + 128] = turned[size_y - radius :]
        return carry

    lax.fori_loop(0, len(fields), filtered, 0)


def along_x_last(fields, before, own, after, partial):
    _, z, x, y = own.shape
    count = len(fields)

    def kernel(*refs):
        last_kernel(fields, *refs)

    return pl.pallas_call(
        kernel,
        out_shape=(
            jax.ShapeDtypeStruct((count, z * x, y), F32),
            jax.ShapeDtypeStruct((count, FW, z * x), F32),
        ),
        in_specs=[WHOLE] * 4,
        out_specs=(WHOLE, WHOLE),
        scratch_shapes=[pltpu.VMEM((count, z + FW, x, y), F32), pltpu.VMEM((z, 2 * x, y), F32)],
        compiler_params=PARAMS,
        cost_estimate=pl.CostEstimate(flops=count * z * x * y * 100, bytes_accessed=40 * z * x * y * 4, transcendentals=0),
    )(before, own, after, partial)


def hat(size, row, offset):
    distance = lax.broadcasted_iota(jnp.int32, (size, row.shape[1]), 0) - row
    return jnp.where(distance == 0, 1.0 - offset, jnp.where(distance == 1, offset, 0.0))


def hat_kernel(sizes, asked, w_high, w_low, w_y):
    size_z, size_x, size_y = sizes
    blocks = asked.shape[2] // BLOCK

    def weights(n, carry):
        group = n // blocks
        here = pl.ds(pl.multiple_of((n % blocks) * BLOCK, BLOCK), BLOCK)
        there = pl.ds(pl.multiple_of(n * BLOCK, BLOCK), BLOCK)
        cell = asked[group, 0:1, here].astype(jnp.int32)
        wx, wy, wz = (asked[group, k : k + 1, here] for k in (1, 2, 3))
        in_z = hat(size_z, cell // (size_x * size_y), wz)
        in_x = hat(size_x, (cell // size_y) % size_x, wx)
        w_y[:, there] = hat(size_y, cell % size_y, wy)
        for z in range(size_z):
            high, low = split2(in_z[z : z + 1] * in_x)
            w_high[z * size_x : (z + 1) * size_x, there] = high
            w_low[z * size_x : (z + 1) * size_x, there] = low
        return carry

    lax.fori_loop(0, asked.shape[0] * blocks, weights, 0)


def hats(asked, sizes):
    size_z, size_x, size_y = sizes
    count = asked.shape[0] * asked.shape[2]

    def kernel(*refs):
        hat_kernel(sizes, *refs)

    return pl.pallas_call(
        kernel,
        out_shape=(
            jax.ShapeDtypeStruct((size_z * size_x, count), BF16),
            jax.ShapeDtypeStruct((size_z * size_x, count), BF16),
            jax.ShapeDtypeStruct((size_y, count), F32),
        ),
        in_specs=[WHOLE],
        out_specs=(WHOLE,) * 3,
        compiler_params=PARAMS,
        cost_estimate=pl.CostEstimate(flops=count * 2000, bytes_accessed=count * 1600, transcendentals=0),
    )(asked)


def y_kernel(band, fields, *refs):
    out = refs[-1]

    def filtered(f, carry):
        total = lax.dot_general(
            band[...], fields[f], (((1,), (1,)), ((), ())),
            precision=lax.Precision.HIGHEST, preferred_element_type=F32,
        )
        if len(refs) > 1:
            total = total + jnp.dot(
                refs[0][...], refs[1][f], precision=lax.Precision.HIGHEST, preferred_element_type=F32
            )
        out[f] = total
        return carry

    lax.fori_loop(0, fields.shape[0], filtered, 0)


def along_y(band, fields, *edges):
    count, cells, size_y = fields.shape
    return pl.pallas_call(
        y_kernel,
        out_shape=jax.ShapeDtypeStruct((count, size_y, cells), F32),
        in_specs=[WHOLE] * (2 + len(edges)),
        out_specs=WHOLE,
        compiler_params=PARAMS,
        cost_estimate=pl.CostEstimate(flops=count * 12 * size_y * size_y * cells, bytes_accessed=2 * count * cells * size_y * 4, transcendentals=0),
    )(band, fields, *edges)


def sample_kernel(first, partial, strips, band, w_high, w_low, w_y, out, field_high, field_low):
    size_y = partial.shape[1]
    blocks = out.shape[2] // BLOCK

    def smooth(f):
        done = first.shape[0]
        if f < done:
            return first[f]
        return partial[f - done] + jnp.dot(
            band[...], strips[f - done], precision=lax.Precision.HIGHEST, preferred_element_type=F32
        )

    mean = [smooth(k) for k in range(3)]
    for k, (a, b) in enumerate(PAIRS):
        high, low = split2(smooth(3 + k) - mean[a] * mean[b])
        field_high[k * size_y : (k + 1) * size_y] = high
        field_low[k * size_y : (k + 1) * size_y] = low

    def sample(n, carry):
        group = n // blocks
        here = pl.ds(pl.multiple_of((n % blocks) * BLOCK, BLOCK), BLOCK)
        there = pl.ds(pl.multiple_of(n * BLOCK, BLOCK), BLOCK)
        high = w_high[:, there]
        wide = jnp.dot(field_high[...], high, preferred_element_type=F32)
        wide = wide + jnp.dot(field_low[...], high, preferred_element_type=F32)
        wide = wide + jnp.dot(field_high[...], w_low[:, there], preferred_element_type=F32)
        in_y = w_y[:, there]
        for k in range(6):
            part = wide[k * size_y : (k + 1) * size_y] * in_y
            out[group, k : k + 1, here] = jnp.sum(part, axis=0, keepdims=True)
        out[group, 6:ROWS, here] = jnp.zeros((ROWS - 6, BLOCK), F32)
        return carry

    lax.fori_loop(0, out.shape[0] * blocks, sample, 0, unroll=16)


def samples(first, partial, strips, band, w_high, w_low, w_y, groups):
    _, size_y, cells = partial.shape
    count = w_y.shape[1]
    return pl.pallas_call(
        sample_kernel,
        out_shape=jax.ShapeDtypeStruct((groups, ROWS, count // groups), F32),
        in_specs=[WHOLE] * 7,
        out_specs=WHOLE,
        scratch_shapes=[pltpu.VMEM((6 * size_y, cells), BF16), pltpu.VMEM((6 * size_y, cells), BF16)],
        compiler_params=PARAMS,
        cost_estimate=pl.CostEstimate(flops=6 * size_y * cells * count * 6, bytes_accessed=8 * 1024 * 1024, transcendentals=0),
    )(first, partial, strips, band, w_high, w_low, w_y)


def route_kernel(owners, capacity, record, out, slot_out, target_out):
    count = record.shape[1]
    target = record[0:1].astype(jnp.int32)
    named = lax.broadcasted_iota(jnp.int32, (owners, count), 0) == target
    earlier = lax.broadcasted_iota(jnp.int32, (count, count), 0) < lax.broadcasted_iota(jnp.int32, (count, count), 1)
    before = jnp.dot(
        jnp.where(named, 1.0, 0.0).astype(BF16), jnp.where(earlier, 1.0, 0.0).astype(BF16),
        preferred_element_type=F32,
    )
    rank = jnp.sum(jnp.where(named, before, 0.0), axis=0, keepdims=True).astype(jnp.int32)
    target_out[...] = target
    slot = lax.broadcasted_iota(jnp.int32, (capacity, count), 0) == rank
    slot = jnp.where(slot, 1.0, 0.0).astype(BF16)
    slot_out[...] = slot
    total = jnp.zeros((owners * 8, capacity), F32)
    for part in split3(record[...]):
        part = part.astype(F32)
        spread = jnp.concatenate(
            [jnp.where(target == o, part, 0.0) for o in range(owners)], axis=0
        ).astype(BF16)
        total = total + lax.dot_general(spread, slot, (((1,), (1,)), ((), ())), preferred_element_type=F32)
    for o in range(owners):
        out[o] = total[o * 8 + 1 : o * 8 + 5]


def route(record, owners, capacity):
    count = record.shape[1]

    def kernel(*refs):
        route_kernel(owners, capacity, *refs)

    return pl.pallas_call(
        kernel,
        out_shape=(
            jax.ShapeDtypeStruct((owners, 4, capacity), F32),
            jax.ShapeDtypeStruct((capacity, count), BF16),
            jax.ShapeDtypeStruct((1, count), jnp.int32),
        ),
        in_specs=[WHOLE],
        out_specs=(WHOLE,) * 3,
        compiler_params=PARAMS,
        cost_estimate=pl.CostEstimate(flops=10 * count * count * owners, bytes_accessed=count * 4 * 40, transcendentals=0),
    )(record)


def return_kernel(owners, back, slot, owner, out):
    count = owner.shape[1]
    picked = jnp.zeros((owners * ROWS, count), F32)
    for part in split2(back[...]):
        picked = picked + jnp.dot(part, slot[...], preferred_element_type=F32)
    target = owner[...]
    total = jnp.zeros((ROWS, count), F32)
    for o in range(owners):
        total = total + jnp.where(target == o, picked[o * ROWS : (o + 1) * ROWS], 0.0)
    out[...] = total[:6]


def returned(back, slot, owner, owners):
    count = owner.shape[1]

    def kernel(*refs):
        return_kernel(owners, *refs)

    return pl.pallas_call(
        kernel,
        out_shape=jax.ShapeDtypeStruct((6, count), F32),
        in_specs=[WHOLE] * 3,
        out_specs=WHOLE,
        compiler_params=PARAMS,
        cost_estimate=pl.CostEstimate(flops=6 * owners * ROWS * back.shape[1] * count, bytes_accessed=count * 100, transcendentals=0),
    )(back, slot, owner)


def y_band(size_y):
    radius = FW // 2
    place = np.concatenate([np.arange(size_y + radius), np.arange(-radius, 0)])
    offset = place[None, :] - np.arange(size_y)[:, None] + radius
    g = np.array(taps())
    band = np.where((offset >= 0) & (offset <= FW), g[np.clip(offset, 0, FW)], 0.0)
    return band[:, :size_y].astype(np.float32), band[:, size_y:].astype(np.float32)


def y_strips(edges):
    radius = FW // 2
    devices = lax.axis_size("gy")
    if devices == 2:
        return lax.ppermute(edges, "gy", [(0, 1), (1, 0)])
    following = shifted(edges[:, :radius], "gy", -1)
    previous = shifted(edges[:, radius:], "gy", 1)
    return jnp.concatenate([following, previous], axis=1)


def on_device(velocity, owner, cell_x, cell_y, cell_z, query_weights):
    _, size_z, size_x, size_y = velocity.shape
    owners = lax.axis_size("gx") * lax.axis_size("gy")
    count = owner.shape[0]
    capacity = 4 * count // owners

    sizes = (size_z, size_x, size_y)
    folded = capacity % BLOCK != 0

    sizes = (size_z, size_x, size_y)
    folded = capacity % BLOCK != 0

    row = lax.broadcasted_iota(jnp.int32, (8, count), 0)
    flat = (jnp.broadcast_to(k.reshape(1, count), (8, count)) for k in (owner, cell_x, cell_y, cell_z))
    named, in_x, in_y, in_z = flat
    cell = (in_z * size_x + in_x) * size_y + in_y
    record = jnp.pad(query_weights, ((2, 3), (0, 0)))
    record = jnp.where(row > 1, record, jnp.where(row == 1, cell, named).astype(F32))
    sent, slot, target = route(record, owners, capacity)

    right = shifted(velocity, "gx", -1)
    left = shifted(after(velocity, record), "gx", 1)
    own_halo = shifted(velocity, "gz", 1), shifted(after(velocity, record), "gz", -1)
    right = relayed(right)
    asked = lax.all_to_all(sent, ("gx", "gy"), split_axis=0, concat_axis=0, tiled=True)
    own_z = along_z(own_halo[0], velocity, own_halo[1])
    left = (shifted(after(left, own_z, asked), "gz", 1), left, shifted(own_halo[1], "gx", 1))
    partial = along_x_first(own_z, along_z(*right))
    if folded:
        asked = asked.transpose(1, 0, 2).reshape(1, 4, owners * capacity)
    weights = hats(asked, sizes)
    partial = after(partial, weights)
    band_own, band_strips = y_band(size_y)
    first, edges = along_x_last(tuple(range(4)), *left, partial)
    first_strips = y_strips(edges)
    second, edges = along_x_last(tuple(range(4, 9)), *left, partial)
    second_strips = y_strips(edges)
    band_own, band_strips = jnp.asarray(band_own), jnp.asarray(band_strips)
    partial = along_y(band_own, second)
    whole = along_y(band_own, after(first, partial), band_strips, first_strips)
    values = samples(whole, partial, second_strips, band_strips, *weights, asked.shape[0])
    if folded:
        values = values.reshape(ROWS, owners, capacity).transpose(1, 0, 2)
    back = lax.all_to_all(values, ("gx", "gy"), split_axis=0, concat_axis=0, tiled=True)
    return returned(back.reshape(owners * ROWS, capacity), slot, target, owners)


def solution(mesh):
    placed = (
        P(None, "gz", "gx", "gy"),
        P(("gx", "gy", "gz"), None),
        P(("gx", "gy", "gz")),
        P(("gx", "gy", "gz")),
        P(("gx", "gy", "gz")),
        P(None, ("gx", "gy", "gz")),
    )
    return jax.shard_map(
        on_device,
        mesh=mesh,
        in_specs=placed,
        out_specs=P(None, ("gx", "gy", "gz")),
        check_vma=False,
    )
```
